32 devices in a mesh: gx: 8 (over z, y), gy: 4 (over x, core).
Axes of the slice: x: 2, y: 2, z: 4, core: 2. Of those that a mesh axis runs over, the one named last changes fastest.
Arguments:
- wavefield: bfloat16 [2, 1, 3584, 1792], P(None, None, 'gx', 'gy'), may hold values from -6 to 6
- slowness: float32 [3584, 1792], P('gx', 'gy'), may hold values from -4 to 4
- frequencies: float32 [1], replicated, may hold values from 1 to 4
- propagator: bfloat16 [3, 1, 2, 256, 256], replicated, may hold values from -0.25 to 0.25
- window_velocity_group: int32 [16, 8], replicated, may hold values from 0 to 2
- reach_list: int32 [16, 8, 5], replicated, may hold values from -1 to 127, as said below
- coupling: float32 [16, 8, 5, 2], replicated, may hold values from -3 to 3
Outputs:
- migrated: bfloat16 [2, 1, 3584, 1792], P(None, None, 'gx', 'gy')
The draws below stay inside these ranges and needn't reach their ends.
Inputs may be any that keep to these rules, and one draw needn't show every extreme that they name: `reach_list`: slot 0 of window (x, y) holds the window itself, x * 8 + y. Every other slot holds -1 or one of the eight windows that touch (x, y) along x, y or a diagonal; the entries of one list are distinct apart from -1. Some windows have one live entry, some have 5.
All inputs are finite; a program needn't handle non-finite values.
Results may differ from the reference program's by a relative error of at most 0.01.
Values may be sent and summed in bfloat16 or wider, within the bound.
No kernel may reach another device: no remote copies, remote signals or barrier semaphores. Data moves between devices by JAX's collectives and lax.ppermute only.
A program may use at most 64 MiB of HBM per device.

```python
import math
import jax
import jax.numpy as jnp
from jax import lax

WINDOW_CELLS = 256
OVER = 32
FREQUENCY_COUNT = 1
VELOCITY_GROUPS = 3
SLOTS = 5
WINDOWS_ALONG_X = 16
WINDOWS_ALONG_Y = 8
NX = 3584
NY = 1792


def draw_reach_list(key, part):
    base_key = jax.random.fold_in(key, 7)
    count_key, order_key = jax.random.split(base_key, 2)
    counts = jax.random.randint(count_key, (WINDOWS_ALONG_X, WINDOWS_ALONG_Y), 1, SLOTS + 1)
    counts = counts.at[0, 0].set(1).at[WINDOWS_ALONG_X - 1, WINDOWS_ALONG_Y - 1].set(SLOTS)
    scores = jax.random.randint(order_key, (WINDOWS_ALONG_X, WINDOWS_ALONG_Y, 8), 0, 1 << 20) * 8 + jnp.arange(8)
    ordering = jnp.argsort(scores, axis=-1)[..., :SLOTS - 1]
    offset_x = jnp.array([-1, -1, -1, 0, 0, 1, 1, 1], dtype=jnp.int32)
    offset_y = jnp.array([-1, 0, 1, -1, 1, -1, 0, 1], dtype=jnp.int32)
    neighbour_x = jnp.arange(WINDOWS_ALONG_X)[:, None, None] + offset_x[ordering]
    neighbour_y = jnp.arange(WINDOWS_ALONG_Y)[None, :, None] + offset_y[ordering]
    inside = (neighbour_x >= 0) & (neighbour_x < WINDOWS_ALONG_X) & (neighbour_y >= 0) & (neighbour_y < WINDOWS_ALONG_Y)
    wanted = (jnp.arange(1, SLOTS)[None, None, :] < counts[:, :, None]) & inside
    others = jnp.where(wanted, neighbour_x * WINDOWS_ALONG_Y + neighbour_y, -1)
    itself = (jnp.arange(WINDOWS_ALONG_X)[:, None] * WINDOWS_ALONG_Y + jnp.arange(WINDOWS_ALONG_Y)[None, :])[:, :, None]
    return jnp.concatenate([itself, others], axis=2).astype(jnp.int32)


def set_ends(entries, key, smallest, largest):
    shape = entries.shape
    index_at = [jax.random.randint(jax.random.fold_in(key, axis), (), 0, shape[axis]) for axis in range(len(shape))]
    entries = entries.at[tuple(index_at)].set(smallest)
    longest = shape.index(max(shape))
    index_at[longest] = (index_at[longest] + 1) % shape[longest]
    return entries.at[tuple(index_at)].set(largest)


def block_scale(rng, dims, shards, least, largest):
    def one(dim, parts):
        heights = jax.random.uniform(jax.random.fold_in(jax.random.fold_in(rng, 6), dim), (parts,), jnp.float32, least / len(shards), largest / len(shards))
        return jnp.repeat(jnp.exp(heights), dims[dim] // parts).reshape((-1,) + (1,) * (len(dims) - dim - 1))

    gain = one(*shards[0])
    for cut in shards[1:]:
        gain = gain * one(*cut)
    return gain


def gaussian(key, extent, scale, bound, cuts=(), kind=jnp.bfloat16):
    gain = block_scale(key, extent, cuts, -0.22, 0.18) if cuts else 1.0
    values = jax.random.normal(key, extent, jnp.float32) * scale * gain
    return jnp.minimum(jnp.maximum(values, -bound), bound).astype(kind)


def setup_inputs(seed: int = 0) -> dict:
    key_list = jax.random.split(jax.random.key(seed), 8)
    return {
        "wavefield": gaussian(key_list[0], (2, FREQUENCY_COUNT, NX, NY), 1.0, 6.0, ((2, 8), (3, 4))),
        "slowness": gaussian(key_list[1], (NX, NY), 0.6, 4.0, ((0, 8), (1, 4)), jnp.float32),
        "frequencies": jnp.clip(jax.random.uniform(key_list[2], (FREQUENCY_COUNT,), jnp.float32, 1.0, 4.0), 1.0, 4.0),
        "propagator": gaussian(key_list[3], (VELOCITY_GROUPS, FREQUENCY_COUNT, 2, WINDOW_CELLS, WINDOW_CELLS), (2 * WINDOW_CELLS) ** -0.5, 0.25),
        "window_velocity_group": set_ends(jax.random.randint(key_list[4], (WINDOWS_ALONG_X, WINDOWS_ALONG_Y), 0, VELOCITY_GROUPS), jax.random.fold_in(key_list[4], 1), 0, VELOCITY_GROUPS - 1).astype(jnp.int32),
        "reach_list": draw_reach_list(jax.random.fold_in(key_list[7], 71), 0),
        "coupling": gaussian(key_list[6], (WINDOWS_ALONG_X, WINDOWS_ALONG_Y, SLOTS, 2), 0.5, 3.0, (), jnp.float32),
    }


def cosine_table(length):
    points = jnp.arange(length, dtype=jnp.float32) + 0.5
    return jnp.sqrt(2.0 / length) * jnp.cos(math.pi / length * points[:, None] * points[None, :])

def bell_curve(length, margin):
    points = jnp.arange(length, dtype=jnp.float32)
    rising = jnp.sin(0.5 * math.pi * (points + 0.5) / margin)
    falling = jnp.cos(0.5 * math.pi * (points - (length - margin) + 0.5) / margin)
    return jnp.where(points < margin, rising, jnp.where(points >= length - margin, falling, 1.0))

def rounded(values):
    return lax.optimization_barrier(values.astype(jnp.bfloat16))

def complex_apply(spec, matrix_real, matrix_imag, data_real, data_imag):

    def contract(left, right):
        return jnp.einsum(spec, left.astype(jnp.float32), right.astype(jnp.float32))
    real_part = contract(matrix_real, data_real) - contract(matrix_imag, data_imag)
    imag_part = contract(matrix_real, data_imag) + contract(matrix_imag, data_real)
    return rounded(jnp.stack([real_part, imag_part]))

def one_frequency(wave_slice, prop_slice, angular, slowness, window_velocity_group, reach_list, coupling):
    half_rim = OVER // 2
    stride = WINDOW_CELLS - OVER
    cosines = rounded(cosine_table(WINDOW_CELLS)).astype(jnp.float32)
    bell_values = bell_curve(WINDOW_CELLS, OVER)
    padded = jnp.pad(wave_slice, ((0, 0), (half_rim, half_rim), (half_rim, half_rim)))
    row_cells = (jnp.arange(WINDOWS_ALONG_X) * stride)[:, None] + jnp.arange(WINDOW_CELLS)[None, :]
    col_cells = (jnp.arange(WINDOWS_ALONG_Y) * stride)[:, None] + jnp.arange(WINDOW_CELLS)[None, :]
    patches = padded[:, row_cells][:, :, :, col_cells]
    tapered = rounded(patches.astype(jnp.float32) * bell_values[None, None, :, None, None] * bell_values)
    first_pass = rounded(jnp.einsum('lb,pxayb->pxayl', cosines, tapered.astype(jnp.float32)))
    coefficients = rounded(jnp.einsum('ka,pxayl->pxkyl', cosines, first_pass.astype(jnp.float32)))
    chosen = prop_slice[window_velocity_group]
    swept_coefs = complex_apply('xymk,xkyl->xmyl', chosen[:, :, 0], chosen[:, :, 1], coefficients[0], coefficients[1])
    by_window = jnp.transpose(swept_coefs, (0, 1, 3, 2, 4)).reshape(2, WINDOWS_ALONG_X * WINDOWS_ALONG_Y, WINDOW_CELLS, WINDOW_CELLS).astype(jnp.float32)
    is_live = reach_list >= 0
    safe_index = jnp.where(is_live, reach_list, 0)
    scale_real = jnp.where(is_live, coupling[..., 0], 0.0)
    scale_imag = jnp.where(is_live, coupling[..., 1], 0.0)
    mixed_real = jnp.zeros((WINDOWS_ALONG_X, WINDOWS_ALONG_Y, WINDOW_CELLS, WINDOW_CELLS), jnp.float32)
    mixed_imag = jnp.zeros((WINDOWS_ALONG_X, WINDOWS_ALONG_Y, WINDOW_CELLS, WINDOW_CELLS), jnp.float32)
    for slot_index in range(SLOTS):
        picked = by_window[:, safe_index[:, :, slot_index]]
        weight_real = scale_real[:, :, slot_index][:, :, None, None]
        weight_imag = scale_imag[:, :, slot_index][:, :, None, None]
        mixed_real = mixed_real + weight_real * picked[0] - weight_imag * picked[1]
        mixed_imag = mixed_imag + weight_real * picked[1] + weight_imag * picked[0]
    mixed_coefs = rounded(jnp.stack([mixed_real, mixed_imag]))
    propagated = complex_apply('xynl,xykl->xykn', chosen[:, :, 0], chosen[:, :, 1], mixed_coefs[0], mixed_coefs[1])
    second = rounded(jnp.einsum('lb,pxykl->pxykb', cosines, propagated.astype(jnp.float32)))
    pieces = jnp.einsum('ka,pxykb->pxayb', cosines, second.astype(jnp.float32))
    pieces = pieces * bell_values[None, None, :, None, None] * bell_values
    canvas = jnp.zeros((2, WINDOWS_ALONG_X * stride + OVER, WINDOWS_ALONG_Y * stride + OVER), jnp.float32)
    canvas = canvas.at[:, row_cells[:, :, None, None], col_cells[None, None, :, :]].add(pieces)
    summed = canvas[:, half_rim:half_rim + WINDOWS_ALONG_X * stride, half_rim:half_rim + WINDOWS_ALONG_Y * stride]
    phases = angular * slowness
    cos_phase = jnp.cos(phases)
    sin_phase = jnp.sin(phases)
    out_real = summed[0] * cos_phase - summed[1] * sin_phase
    out_imag = summed[0] * sin_phase + summed[1] * cos_phase
    return jnp.stack([out_real, out_imag]).astype(jnp.bfloat16)

def reference(wavefield, slowness, frequencies, propagator, window_velocity_group, reach_list, coupling):

    def per_frequency(inputs):
        wave_slice, prop_slice, angular = inputs
        return one_frequency(wave_slice, prop_slice, angular, slowness, window_velocity_group, reach_list, coupling)
    results = lax.map(per_frequency, (jnp.transpose(wavefield, (1, 0, 2, 3)), jnp.transpose(propagator, (1, 0, 2, 3, 4)), frequencies))
    return jnp.transpose(results, (1, 0, 2, 3))
```

```python
import math

import jax
import jax.numpy as jnp
import ml_dtypes
import numpy as np
from jax import lax
from jax.experimental import pallas as pl
from jax.experimental.pallas import tpu as pltpu
from jax.sharding import PartitionSpec as P

OVER = 32
HALF = OVER // 2
F32 = jnp.float32
BF16 = jnp.bfloat16
VMEM = pl.BlockSpec(memory_space=pltpu.VMEM)
SMEM = pl.BlockSpec(memory_space=pltpu.SMEM)
PARAMS = pltpu.CompilerParams(vmem_limit_bytes=48 * 2**20)


def cosine_table(length):
    points = np.arange(length, dtype=np.float32) + np.float32(0.5)
    angles = (np.float32(math.pi / length) * points[:, None]) * points[None, :]
    waves = np.cos(angles.astype(np.float64)).astype(np.float32)
    return (np.sqrt(np.float32(2.0 / length)) * waves).astype(ml_dtypes.bfloat16)


def bell_curve(length, margin):
    points = np.arange(length, dtype=np.float64)
    rising = np.sin(0.5 * math.pi * (points + 0.5) / margin)
    falling = np.cos(0.5 * math.pi * (points - (length - margin) + 0.5) / margin)
    bell = np.where(points < margin, rising, np.where(points >= length - margin, falling, 1.0))
    return bell.astype(np.float32)


def dot(left, right):
    return jnp.dot(left, right, preferred_element_type=F32)


def swap(block, axis, odd):
    size = lax.axis_size(axis)
    pairs = []
    for i in range(1 if odd else 0, size - 1, 2):
        pairs += [(i, i + 1), (i + 1, i)]
    return lax.ppermute(block, axis, pairs)


def parity(axis):
    return lax.rem(lax.axis_index(axis), 2)


def folded_kernel(prop_ref, cos_ref, cos_t_ref, row_ref, col_ref, left_ref, right_ref):
    groups, _, _, length, _ = prop_ref.shape
    wide = right_ref.shape[-1]
    bell = col_ref[...] * row_ref[...]
    inner = wide - 2 * OVER
    for g in range(groups):
        for part in range(2):
            half = dot(prop_ref[g, 0, part], cos_ref[...])
            high = half.astype(BF16)
            low = (half - high.astype(F32)).astype(BF16)
            full = (dot(cos_t_ref[...], high) + dot(cos_t_ref[...], low)) * bell
            left_ref[g, part] = full
            flipped = full.T
            zeros = jnp.zeros((length, wide), F32)
            edge = length - HALF
            right_ref[g, 0, part] = jnp.concatenate(
                [
                    flipped[:, HALF:],
                    zeros[:, : inner - edge],
                    flipped[:, :HALF],
                    zeros[:, : wide - inner - HALF],
                ],
                axis=1,
            ).astype(BF16)
            right_ref[g, 1, part] = jnp.concatenate(
                [
                    zeros[:, : inner - edge],
                    flipped[:, :edge],
                    zeros[:, :HALF],
                    flipped[:, edge:],
                    zeros[:, : wide - inner - OVER],
                ],
                axis=1,
            ).astype(BF16)


def fold(propagator, cosines, bell):
    groups, _, _, length, _ = propagator.shape
    wide = 2 * length
    return pl.pallas_call(
        folded_kernel,
        out_shape=(
            jax.ShapeDtypeStruct((groups, 2, length, length), F32),
            jax.ShapeDtypeStruct((groups, 2, 2, length, wide), BF16),
        ),
        in_specs=[VMEM] * 5,
        out_specs=(VMEM, VMEM),
        compiler_params=PARAMS,
        name="fold",
    )(propagator, cosines, cosines.T, bell[None, :], bell[:, None])


def spread(frame_ref, start, left, middle, right):
    count = middle.shape[1]
    span = left.shape[2]
    rows = pl.ds(start, count)
    wide = middle.shape[2]
    for part in range(2):
        west, centre, east = left[part], middle[part], right[part]
        frame_ref[0, part, rows] = jnp.concatenate([west, centre[:, :HALF]], axis=1)
        frame_ref[1, part, rows] = jnp.concatenate([west[:, span - HALF :], centre[:, :span]], axis=1)
        frame_ref[2, part, rows] = jnp.concatenate([centre[:, wide - span :], east[:, :HALF]], axis=1)
        frame_ref[3, part, rows] = jnp.concatenate([centre[:, wide - HALF :], east], axis=1)


def main_kernel(
    reach_ref,
    coup_ref,
    group_ref,
    own_ref,
    ye_ref,
    yo_ref,
    xe_ref,
    xo_ref,
    ze_ref,
    zo_ref,
    left_ref,
    right_ref,
    mid_ref,
    send_e_ref,
    send_o_ref,
    frame_ref,
    acc_ref,
    total_y,
    slots,
):
    length = left_ref.shape[-1]
    tile = own_ref.shape[1]
    span = length - HALF
    stride = length - OVER
    odd_x, odd_y = parity("gx"), parity("gy")
    base_x = lax.axis_index("gx") * 2
    base_y = lax.axis_index("gy") * 2
    row_e = pl.multiple_of(jnp.where(odd_x == 0, span + tile, 0), HALF)
    row_o = pl.multiple_of(jnp.where(odd_x == 0, 0, span + tile), HALF)

    def place(west, east, west_z, east_z):
        spread(frame_ref, span, west, own_ref, east)
        spread(frame_ref, row_e, west_z.at[:, :span], xe_ref, east_z.at[:, :span])
        spread(frame_ref, row_o, west_z.at[:, span:], xo_ref, east_z.at[:, span:])

    @pl.when(odd_y == 0)
    def _():
        place(yo_ref, ye_ref, zo_ref, ze_ref)

    @pl.when(odd_y == 1)
    def _():
        place(ye_ref, yo_ref, ze_ref, zo_ref)

    acc_ref[...] = jnp.zeros_like(acc_ref)

    def step(index, carry):
        target = index // slots
        slot = index % slots
        window = (base_x + target // 2) * total_y + base_y + target % 2
        source = reach_ref[window * slots + slot]

        @pl.when(source >= 0)
        def _():
            at_x = source // total_y - base_x + 1
            at_y = source % total_y - base_y + 1
            rows = pl.ds(pl.multiple_of(at_x * stride, HALF), length)
            group = group_ref[source]
            w_real = coup_ref[(window * slots + slot) * 2]
            w_imag = coup_ref[(window * slots + slot) * 2 + 1]
            t_real, t_imag = left_ref[group, 0], left_ref[group, 1]
            m_real = (w_real * t_real - w_imag * t_imag).astype(BF16)
            m_imag = (w_real * t_imag + w_imag * t_real).astype(BF16)
            x_real = frame_ref[at_y, 0, rows]
            x_imag = frame_ref[at_y, 1, rows]
            acc_ref[target, 0] += dot(m_real, x_real) - dot(m_imag, x_imag)
            acc_ref[target, 1] += dot(m_real, x_imag) + dot(m_imag, x_real)

        return carry

    lax.fori_loop(0, 4 * slots, step, 0)

    inner = tile
    edge = span
    for row in range(2):
        real = jnp.zeros((length, right_ref.shape[-1]), F32)
        imag = real
        for col in range(2):
            group = group_ref[(base_x + row) * total_y + base_y + col]
            m_real = acc_ref[row * 2 + col, 0].astype(BF16)
            m_imag = acc_ref[row * 2 + col, 1].astype(BF16)
            r_real, r_imag = right_ref[group, col, 0], right_ref[group, col, 1]
            real += dot(m_real, r_real) - dot(m_imag, r_imag)
            imag += dot(m_real, r_imag) + dot(m_imag, r_real)
        for part, out in ((0, real), (1, imag)):
            if row == 0:
                mid_ref[part, :edge] = out[HALF:]
                border = out[:HALF].astype(BF16)
            else:
                both = edge - (inner - edge)
                mid_ref[part, inner - edge : edge] += out[:both]
                mid_ref[part, edge:] = out[both:edge]
                border = out[edge:].astype(BF16)

            @pl.when(odd_x == row)
            def _():
                send_o_ref[part] = border

            @pl.when(odd_x != row)
            def _():
                send_e_ref[part] = border


def border_kernel(mid_ref, got_e_ref, got_o_ref, send_e_ref, send_o_ref, work_ref):
    tile = mid_ref.shape[1]
    odd_x, odd_y = parity("gx"), parity("gy")
    row_e = pl.multiple_of(jnp.where(odd_x == 0, tile - HALF, 0), HALF)
    row_o = pl.multiple_of(jnp.where(odd_x == 0, 0, tile - HALF), HALF)
    work_ref[...] = mid_ref[...]
    at = tile % 128
    for part in range(2):
        work_ref[part, pl.ds(row_e, HALF)] += got_e_ref[part].astype(F32)
        work_ref[part, pl.ds(row_o, HALF)] += got_o_ref[part].astype(F32)
        turned = work_ref[part].T
        west = turned[at : at + HALF].astype(BF16)
        east = turned[at + HALF : at + OVER].astype(BF16)

        @pl.when(odd_y == 0)
        def _():
            send_e_ref[part] = east
            send_o_ref[part] = west

        @pl.when(odd_y == 1)
        def _():
            send_e_ref[part] = west
            send_o_ref[part] = east


def final_kernel(
    mid_ref, xe_ref, xo_ref, ye_ref, yo_ref, cos_ref, sin_ref, out_ref, work_ref
):
    tile = mid_ref.shape[1]
    odd_x, odd_y = parity("gx"), parity("gy")
    row_e = pl.multiple_of(jnp.where(odd_x == 0, tile - HALF, 0), HALF)
    row_o = pl.multiple_of(jnp.where(odd_x == 0, 0, tile - HALF), HALF)
    far = tile - HALF
    lane = lax.broadcasted_iota(jnp.int32, (HALF, tile), 1)
    line = lax.broadcasted_iota(jnp.int32, (HALF, tile), 0)
    pick_e = (lane == line + jnp.where(odd_y == 0, far, 0)).astype(F32).astype(BF16)
    pick_o = (lane == line + jnp.where(odd_y == 0, 0, far)).astype(F32).astype(BF16)

    def outer(values, pick):
        return lax.dot_general(values, pick, (((0,), (0,)), ((), ())), preferred_element_type=F32)

    for part in range(2):
        work_ref[part] = (
            mid_ref[part, :, :tile] + outer(ye_ref[part], pick_e) + outer(yo_ref[part], pick_o)
        )
        work_ref[part, pl.ds(row_e, HALF)] += xe_ref[part, :, :tile].astype(F32)
        work_ref[part, pl.ds(row_o, HALF)] += xo_ref[part, :, :tile].astype(F32)
    real, imag = work_ref[0], work_ref[1]
    out_ref[0, 0] = (real * cos_ref[...] - imag * sin_ref[...]).astype(BF16)
    out_ref[1, 0] = (real * sin_ref[...] + imag * cos_ref[...]).astype(BF16)


def pick_side(odd, first, last, partner_is_even):
    toward_last = odd == (0 if partner_is_even else 1)
    return jnp.where(toward_last, last, first)


def per_device(
    wavefield, slowness, frequencies, propagator, window_velocity_group, reach_list, coupling
):
    length = propagator.shape[-1]
    span = length - HALF
    wide = 2 * length
    tile_rows, tile_cols = wavefield.shape[2:]
    total_y = window_velocity_group.shape[1]
    slots = reach_list.shape[2]
    odd_x, odd_y = parity("gx"), parity("gy")
    own = wavefield[:, 0]
    first_x, last_x = own[:, :span], own[:, tile_rows - span :]
    first_y, last_y = own[:, :, :span], own[:, :, tile_cols - span :]
    x_even = swap(pick_side(odd_x, first_x, last_x, True), "gx", False)
    x_odd = swap(pick_side(odd_x, first_x, last_x, False), "gx", True)
    y_even = swap(pick_side(odd_y, first_y, last_y, True), "gy", False)
    y_odd = swap(pick_side(odd_y, first_y, last_y, False), "gy", True)
    arrived = jnp.concatenate([x_even, x_odd], axis=1)
    first_z, last_z = arrived[:, :, :span], arrived[:, :, tile_cols - span :]
    z_even = swap(pick_side(odd_y, first_z, last_z, True), "gy", False)
    z_odd = swap(pick_side(odd_y, first_z, last_z, False), "gy", True)

    cosines = cosine_table(length)
    bell = bell_curve(length, OVER)
    left, right = fold(propagator, cosines, bell)

    def main(*refs):
        main_kernel(*refs, total_y=total_y, slots=slots)

    mid, send_e, send_o = pl.pallas_call(
        main,
        out_shape=(
            jax.ShapeDtypeStruct((2, tile_rows, wide), F32),
            jax.ShapeDtypeStruct((2, HALF, wide), BF16),
            jax.ShapeDtypeStruct((2, HALF, wide), BF16),
        ),
        in_specs=[SMEM] * 3 + [VMEM] * 9,
        out_specs=(VMEM,) * 3,
        scratch_shapes=[
            pltpu.VMEM((4, 2, tile_rows + 2 * span, length), BF16),
            pltpu.VMEM((4, 2, length, length), F32),
        ],
        compiler_params=PARAMS,
        name="mix",
    )(
        reach_list.reshape(-1),
        coupling.reshape(-1),
        window_velocity_group.reshape(-1),
        own,
        y_even,
        y_odd,
        x_even,
        x_odd,
        z_even,
        z_odd,
        left,
        right,
    )
    rows_e = swap(send_e, "gx", False)
    rows_o = swap(send_o, "gx", True)

    last_block = tile_cols // 128
    side = pl.BlockSpec((2, HALF, 128), lambda i: (0, 0, last_block))
    cols_spec = pl.BlockSpec((2, HALF, tile_rows), lambda i: (0, 0, 0))
    send_e, send_o = pl.pallas_call(
        border_kernel,
        grid=(1,),
        out_shape=(jax.ShapeDtypeStruct((2, HALF, tile_rows), BF16),) * 2,
        in_specs=[pl.BlockSpec((2, tile_rows, 128), lambda i: (0, 0, last_block)), side, side],
        out_specs=(cols_spec, cols_spec),
        scratch_shapes=[pltpu.VMEM((2, tile_rows, 128), F32)],
        compiler_params=PARAMS,
        name="border",
    )(mid, rows_e, rows_o)
    cols_e = swap(send_e, "gy", False)
    cols_o = swap(send_o, "gy", True)

    phases = frequencies[0] * slowness
    return pl.pallas_call(
        final_kernel,
        out_shape=jax.ShapeDtypeStruct(wavefield.shape, BF16),
        in_specs=[VMEM] * 7,
        out_specs=VMEM,
        scratch_shapes=[pltpu.VMEM((2, tile_rows, tile_cols), F32)],
        compiler_params=PARAMS,
        name="turn",
    )(mid, rows_e, rows_o, cols_e, cols_o, jnp.cos(phases), jnp.sin(phases))


def solution(mesh):
    return jax.shard_map(
        per_device,
        mesh=mesh,
        in_specs=(P(None, None, "gx", "gy"), P("gx", "gy"), P(), P(), P(), P(), P()),
        out_specs=P(None, None, "gx", "gy"),
        check_vma=False,
    )
```

```python
import functools
import math

import jax
import jax.numpy as jnp
import ml_dtypes
import numpy as np
from jax import lax
from jax.experimental import pallas as pl
from jax.experimental.pallas import tpu as pltpu
from jax.sharding import PartitionSpec as P

OVER = 32
HALF = OVER // 2
F32 = jnp.float32
BF16 = jnp.bfloat16
VMEM = pl.BlockSpec(memory_space=pltpu.VMEM)
SMEM = pl.BlockSpec(memory_space=pltpu.SMEM)
HBM = pl.BlockSpec(memory_space=pltpu.HBM)
PARAMS = pltpu.CompilerParams(vmem_limit_bytes=20 * 2**20)


def cosine_table(length):
    points = np.arange(length, dtype=np.float32) + np.float32(0.5)
    angles = (np.float32(math.pi / length) * points[:, None]) * points[None, :]
    waves = np.cos(angles.astype(np.float64)).astype(np.float32)
    return (np.sqrt(np.float32(2.0 / length)) * waves).astype(ml_dtypes.bfloat16)


def bell_curve(length, margin):
    points = np.arange(length, dtype=np.float64)
    rising = np.sin(0.5 * math.pi * (points + 0.5) / margin)
    falling = np.cos(0.5 * math.pi * (points - (length - margin) + 0.5) / margin)
    bell = np.where(points < margin, rising, np.where(points >= length - margin, falling, 1.0))
    return bell.astype(np.float32)


def dot(left, right):
    return jnp.dot(left, right, preferred_element_type=F32)


def swap(block, axis, odd):
    size = lax.axis_size(axis)
    pairs = []
    for i in range(1 if odd else 0, size - 1, 2):
        pairs += [(i, i + 1), (i + 1, i)]
    return lax.ppermute(block, axis, pairs)


def parity(axis):
    return lax.rem(lax.axis_index(axis), 2)


def cost(micros):
    return pl.CostEstimate(
        flops=int(micros * 1.1e9), bytes_accessed=int(micros * 3.6e6), transcendentals=0
    )


def fetch(pairs, sems):
    copies = [pltpu.make_async_copy(a, b, sems.at[i]) for i, (a, b) in enumerate(pairs)]
    for copy in copies:
        copy.start()
    return copies


def list_tables(all_reach_ref, all_coup_ref, all_group_ref, table_ref):
    slots, total_y, total_x = all_reach_ref.shape
    odd_x = parity("gx")
    base_x = lax.axis_index("gx") * 2
    base_y = lax.axis_index("gy") * 2
    for row in range(4):
        for col in range(4):
            x = jnp.clip(base_x - 1 + row, 0, total_x - 1)
            y = jnp.clip(base_y - 1 + col, 0, total_y - 1)
            table_ref[row * 4 + col] = all_group_ref[y, x].astype(F32)
    for row in range(3):
        for col in range(2):
            x, y = base_x - odd_x + row, base_y + col
            for slot in range(slots):
                reach = all_reach_ref[slot, y, x]
                place = (reach // total_y - base_x + 1) * 4 + reach % total_y - base_y + 1
                at = 16 + ((row * 2 + col) * slots + slot) * 3
                table_ref[at] = jnp.where(reach >= 0, place, -1).astype(F32)
                table_ref[at + 1] = all_coup_ref[y, slot, 0, x]
                table_ref[at + 2] = all_coup_ref[y, slot, 1, x]


def folded_kernel(
    reach_any,
    coup_any,
    group_any,
    prop_ref,
    cos_ref,
    cos_t_ref,
    row_ref,
    left_ref,
    right_ref,
    strip_ref,
    table_ref,
    reach_ref,
    coup_ref,
    group_ref,
    sems,
):
    pairs = ((reach_any, reach_ref), (coup_any, coup_ref), (group_any, group_ref))
    copies = fetch(pairs, sems)
    groups, _, _, length, _ = prop_ref.shape
    wide = right_ref.shape[-1]
    curve = jnp.broadcast_to(row_ref[...], (length, length))
    bell = curve * curve.T
    inner = wide - 2 * OVER
    edge = length - HALF
    for g in range(groups):
        for part in range(2):
            half = dot(prop_ref[g, 0, part], cos_ref[...])
            high = half.astype(BF16)
            low = (half - high.astype(F32)).astype(BF16)
            full = (dot(cos_t_ref[...], high) + dot(cos_t_ref[...], low)) * bell
            left_ref[g, part] = full
            strip_ref[g, part] = jnp.concatenate([full[:, :HALF], full[:, edge:]], axis=1)
            flipped = full.T
            zeros = jnp.zeros((length, wide), F32)
            right_ref[g, 0, part] = jnp.concatenate(
                [
                    flipped[:, HALF:],
                    zeros[:, : inner - edge],
                    flipped[:, :HALF],
                    zeros[:, : wide - inner - HALF],
                ],
                axis=1,
            ).astype(BF16)
            right_ref[g, 1, part] = jnp.concatenate(
                [
                    zeros[:, : inner - edge],
                    flipped[:, :edge],
                    zeros[:, :HALF],
                    flipped[:, edge:],
                    zeros[:, : wide - inner - OVER],
                ],
                axis=1,
            ).astype(BF16)
    for copy in copies:
        copy.wait()
    list_tables(reach_ref, coup_ref, group_ref, table_ref)


def fold(propagator, cosines, bell, reach_list, coupling, window_velocity_group):
    groups, _, _, length, _ = propagator.shape
    slots = reach_list.shape[2]
    return pl.pallas_call(
        folded_kernel,
        out_shape=(
            pltpu.VMEM((groups, 2, length, length), F32),
            pltpu.VMEM((groups, 2, 2, length, 2 * length), BF16),
            pltpu.VMEM((groups, 2, length, OVER), F32),
            jax.ShapeDtypeStruct((16 + 18 * slots,), F32),
        ),
        in_specs=[pl.BlockSpec(memory_space=pl.ANY)] * 3 + [VMEM] * 4,
        out_specs=(VMEM,) * 3 + (SMEM,),
        scratch_shapes=[
            pltpu.SMEM(reach_list.shape[::-1], jnp.int32),
            pltpu.SMEM(coupling.shape[1:] + coupling.shape[:1], F32),
            pltpu.SMEM(window_velocity_group.shape[::-1], jnp.int32),
            pltpu.SemaphoreType.DMA((3,)),
        ],
        compiler_params=PARAMS,
        cost_estimate=cost(2),
        name="fold",
    )(
        jnp.transpose(reach_list, (2, 1, 0)),
        jnp.transpose(coupling, (1, 2, 3, 0)),
        window_velocity_group.T,
        propagator,
        cosines,
        cosines.T,
        bell[None, :],
    )


def spread(west, middle, east, part):
    span = west.shape[2]
    wide = middle.shape[2]
    left, centre, right = west[part], middle[part], east[part]
    return (
        jnp.concatenate([left, centre[:, :HALF]], axis=1),
        jnp.concatenate([left[:, span - HALF :], centre[:, :span]], axis=1),
        jnp.concatenate([centre[:, wide - span :], right[:, :HALF]], axis=1),
        jnp.concatenate([centre[:, wide - HALF :], right], axis=1),
    )


def each_way(odd, even_call, odd_call):
    pl.when(odd == 0)(even_call)
    pl.when(odd == 1)(odd_call)


def start_of(odd, if_even, if_odd):
    return pl.multiple_of(jnp.where(odd == 0, if_even, if_odd), HALF)


def scaled(table, w_real, w_imag):
    real, imag = table[0], table[1]
    return (
        (w_real * real - w_imag * imag).astype(BF16),
        (w_real * imag + w_imag * real).astype(BF16),
    )


def add_product(out, at, weights, real, imag):
    w_real, w_imag = weights
    out[at + (0,)] += dot(w_real, real) - dot(w_imag, imag)
    out[at + (1,)] += dot(w_real, imag) + dot(w_imag, real)


class Lists:
    def __init__(self, table_ref, slots):
        self.table_ref, self.slots = table_ref, slots
        self.odd_x = parity("gx")

    def group_at(self, place):
        return self.table_ref[place].astype(jnp.int32)

    def window(self, row, col):
        return (row + 1) * 4 + col + 1

    def entry(self, row, col, slot):
        at = 16 + (((row + self.odd_x) * 2 + col) * self.slots + slot) * 3
        reach = self.table_ref[at].astype(jnp.int32)
        return reach, self.table_ref[at + 1], self.table_ref[at + 2]

    def weight_of(self, row, col, source):
        real, imag = jnp.float32(0), jnp.float32(0)
        for slot in range(self.slots):
            reach, c_real, c_imag = self.entry(row, col, slot)
            real += jnp.where(reach == source, c_real, 0.0)
            imag += jnp.where(reach == source, c_imag, 0.0)
        return real, imag

    def slot_of(self, row, col, slot):
        reach, c_real, c_imag = self.entry(row, col, slot)
        live = reach >= 0
        source = jnp.where(live, reach, self.window(row, col))
        at_row = source // 4
        at_x = jnp.where(self.odd_x == 0, at_row, 3 - at_row)
        real = jnp.where(live, c_real, 0.0)
        imag = jnp.where(live, c_imag, 0.0)
        return self.group_at(source), at_x, source % 4, real, imag


def pack_sides(blocks, near_ref, far_ref, part):
    width = near_ref.shape[2]
    start = blocks[0].shape[2] - width

    def store(high_ref, low_ref):
        row = 0
        for block in blocks:
            rows = pl.ds(row, block.shape[1])
            high_ref[part, rows] = block[part, :, start:]
            low_ref[part, rows] = block[part, :, :width]
            row += block.shape[1]

    each_way(parity("gy"), lambda: store(near_ref, far_ref), lambda: store(far_ref, near_ref))


def rows_kernel(wave_ref, x_ref, rim_ref):
    odd_x = parity("gx")
    tile, span = wave_ref.shape[2], x_ref.shape[1]
    for part in range(2):
        x_ref[part] = wave_ref[part, 0, pl.ds(start_of(odd_x, 0, tile - span), span)]
        rim_ref[part] = wave_ref[part, 0, pl.ds(start_of(odd_x, tile - HALF, 0), HALF)]


def cols_kernel(wave_ref, rim_ref, near_ref, far_ref):
    for part in range(2):
        pack_sides([wave_ref.at[:, 0]], near_ref, far_ref, part)


def corner_kernel(x_ref, rim_ref, near_ref, far_ref):
    x_ref = x_ref.at[:, pl.ds(start_of(parity("gx"), HALF, 0), x_ref.shape[1] - HALF)]
    for part in range(2):
        pack_sides([x_ref, rim_ref], near_ref, far_ref, part)


def edge_kernel(lists, wave_ref, ye_ref, yo_ref, left_ref, x_ref, part_ref, frame_ref, sum_ref):
    length = left_ref.shape[-1]
    own_ref = wave_ref.at[:, 0]
    tile = own_ref.shape[1]
    span = length - HALF
    odd_x, odd_y = lists.odd_x, parity("gy")

    def fill(west, east):
        for part in range(2):
            for at, block in enumerate(spread(west, own_ref, east, part)):
                frame_ref[at, part] = block

    each_way(odd_y, lambda: fill(yo_ref, ye_ref), lambda: fill(ye_ref, yo_ref))
    far = tile - span
    low_o, low_e = start_of(odd_x, 0, far), start_of(odd_x, far, 0)
    edge_o, edge_e = start_of(odd_x, 0, tile - HALF), start_of(odd_x, tile - HALF, 0)
    at_o, at_e = start_of(odd_x, HALF, 0), start_of(odd_x, 0, HALF)
    hole_o, hole_e = start_of(odd_x, 0, span), start_of(odd_x, span, 0)
    rim = jnp.zeros((HALF, length), BF16)
    empty = jnp.zeros((length, length), BF16)
    for at in range(4):
        for part in range(2):
            rows = frame_ref.at[at, part]
            x_ref[0, at, part] = empty
            x_ref[3, at, part] = empty
            x_ref[0, at, part, pl.ds(hole_e, HALF)] = rows[pl.ds(edge_o, HALF)]
            x_ref[3, at, part, pl.ds(hole_o, HALF)] = rows[pl.ds(edge_e, HALF)]
            x_ref[1, at, part, pl.ds(at_o, span)] = rows[pl.ds(low_o, span)]
            x_ref[2, at, part, pl.ds(at_e, span)] = rows[pl.ds(low_e, span)]
            x_ref[1, at, part, pl.ds(hole_o, HALF)] = rim
            x_ref[2, at, part, pl.ds(hole_e, HALF)] = rim
    beyond = jnp.where(odd_x == 0, 2, -1)
    mine = jnp.where(odd_x == 0, 1, 0)
    for col in range(2):
        for part in range(2):
            sum_ref[part] = jnp.zeros((length, length), F32)
        for step in range(3):
            source = lists.window(mine, col + step - 1)
            w_real, w_imag = lists.weight_of(beyond, col, source)
            weights = scaled(left_ref.at[lists.group_at(source)], w_real, w_imag)
            add_product(sum_ref, (), weights, x_ref[2, col + step, 0], x_ref[2, col + step, 1])
        for part in range(2):
            part_ref[part, :, col * length : (col + 1) * length] = sum_ref[part].astype(BF16)


def early_kernel(lists, x_ref, left_ref, strip_ref, sum_ref, packed_ref, *, c):
    length = left_ref.shape[-1]
    row = lists.odd_x ^ c
    for col in range(2):
        for part in range(2):
            sum_ref[col, part] = jnp.zeros((length, length), F32)
        strips = []
        for slot in range(lists.slots):
            group, at_x, at_y, w_real, w_imag = lists.slot_of(row, col, slot)
            weights = scaled(left_ref.at[group], w_real, w_imag)
            add_product(sum_ref, (col,), weights, x_ref[at_x, at_y, 0], x_ref[at_x, at_y, 1])
            inside = (at_x == 1) | (at_x == 2)
            w_real = jnp.where(inside, w_real, 0.0)
            w_imag = jnp.where(inside, w_imag, 0.0)
            strips.append(scaled(strip_ref.at[group], w_real, w_imag))
        for part in range(2):
            packed_ref[col, part] = jnp.concatenate([s[part] for s in strips], axis=1)


def late_kernel(
    lists,
    xo_ref,
    rim_ref,
    ze_ref,
    zo_ref,
    left_ref,
    early_o_ref,
    packed_o_ref,
    early_e_ref,
    packed_e_ref,
    right_ref,
    mid_ref,
    send_e_ref,
    send_o_ref,
    outer_ref,
    strip_ref,
    sum_ref,
    out_ref,
):
    length = left_ref.shape[-1]
    span = length - HALF
    tile = mid_ref.shape[1]
    odd_x, odd_y = lists.odd_x, parity("gy")
    at_o, hole_o = start_of(odd_x, 0, HALF), start_of(odd_x, span, 0)
    lean_o, lean_e = start_of(odd_x, 0, HALF), start_of(odd_x, HALF, 0)
    touch = start_of(odd_x, span - HALF, 0)
    xo_ref = xo_ref.at[:, pl.ds(start_of(odd_x, HALF, 0), span)]
    strip_ref[...] = jnp.zeros_like(strip_ref)

    def fill(west, east):
        for part in range(2):
            for at, block in enumerate(spread(west.at[:, :span], xo_ref, east.at[:, :span], part)):
                outer_ref[at, part, pl.ds(at_o, span)] = block
                outer_ref[at, part, pl.ds(hole_o, HALF)] = jnp.zeros((HALF, length), BF16)
            for at, block in enumerate(spread(west.at[:, span:], rim_ref, east.at[:, span:], part)):
                strip_ref[1, at, part, pl.ds(lean_e, HALF)] = block

    each_way(odd_y, lambda: fill(zo_ref, ze_ref), lambda: fill(ze_ref, zo_ref))
    shift = start_of(odd_x, span - HALF, HALF)
    for at in range(4):
        for part in range(2):
            strip_ref[0, at, part, pl.ds(lean_o, HALF)] = outer_ref[at, part, pl.ds(shift, HALF)]

    sum_ref[0] = early_o_ref[...]
    sum_ref[1] = early_e_ref[...]
    beyond = jnp.where(odd_x == 0, -1, 2)
    for c in range(2):
        row = odd_x ^ c
        for col in range(2):
            if c == 0:
                for step in range(3):
                    source = lists.window(beyond, col + step - 1)
                    w_real, w_imag = lists.weight_of(row, col, source)
                    weights = scaled(left_ref.at[lists.group_at(source)], w_real, w_imag)
                    add_product(
                        sum_ref, (c, col), weights, outer_ref[col + step, 0], outer_ref[col + step, 1]
                    )
            rows = [[], []]
            for slot in range(lists.slots):
                _, at_x, at_y, _, _ = lists.slot_of(row, col, slot)
                at_x = jnp.clip(at_x - 1, 0, 1)
                for part in range(2):
                    rows[part].append(strip_ref[at_x, at_y, part])
            real, imag = (jnp.concatenate(r, axis=0) for r in rows)
            packed_ref = packed_o_ref if c == 0 else packed_e_ref
            add_product(sum_ref, (c, col), (packed_ref[col, 0], packed_ref[col, 1]), real, imag)
    mid_ref[...] = jnp.zeros_like(mid_ref)
    for c in range(2):
        row = odd_x ^ c
        groups = [lists.group_at(lists.window(row, col)) for col in range(2)]
        blocks = [[sum_ref[c, col, part].astype(BF16) for part in range(2)] for col in range(2)]
        turn(blocks, right_ref, groups, out_ref)
        lower = odd_x if c == 0 else 1 - odd_x
        source = start_of(lower, HALF, 0)
        target = start_of(lower, 0, tile - span)
        border = start_of(lower, 0, span)
        send = send_o_ref if c == 0 else send_e_ref
        for part in range(2):
            mid_ref[part, pl.ds(target, span)] += out_ref[part, pl.ds(source, span)]
            send[part] = out_ref[part, pl.ds(border, HALF)].astype(BF16)


def turn(blocks, right_ref, groups, out_ref):
    real, imag = 0.0, 0.0
    for col in range(2):
        m_real, m_imag = blocks[col]
        r_real, r_imag = right_ref[groups[col], col, 0], right_ref[groups[col], col, 1]
        real += dot(m_real, r_real) - dot(m_imag, r_imag)
        imag += dot(m_real, r_imag) + dot(m_imag, r_real)
    out_ref[0] = real
    out_ref[1] = imag


def join_kernel(
    lists,
    mid_ref,
    got_ref,
    gave_ref,
    right_ref,
    freq_ref,
    slow_hbm,
    full_ref,
    cos_ref,
    sin_ref,
    out_ref,
    echo_ref,
    slow_ref,
    sems,
):
    copies = fetch([(slow_hbm, slow_ref)], sems)
    length = got_ref.shape[1]
    span = length - HALF
    tile = mid_ref.shape[1]
    odd_x = lists.odd_x

    def halves(ref, rows):
        return [
            [ref[part, rows, col * length : (col + 1) * length] for part in range(2)]
            for col in range(2)
        ]

    mine = jnp.where(odd_x == 0, 1, 0)
    beyond = jnp.where(odd_x == 0, 2, -1)
    groups = [lists.group_at(lists.window(mine, col)) for col in range(2)]
    turn(halves(got_ref, slice(None)), right_ref, groups, out_ref)
    groups = [lists.group_at(lists.window(beyond, col)) for col in range(2)]
    turn(halves(gave_ref, pl.ds(start_of(odd_x, 0, span), HALF)), right_ref, groups, echo_ref)
    source = start_of(odd_x, 0, HALF)
    target = start_of(odd_x, tile - span, 0)
    row_e = start_of(odd_x, tile - HALF, 0)
    full_ref[...] = mid_ref[...]
    for part in range(2):
        full_ref[part, pl.ds(target, span)] += out_ref[part, pl.ds(source, span)]
        full_ref[part, pl.ds(row_e, HALF)] += echo_ref[part]
    copies[0].wait()
    phase(freq_ref, slow_ref, cos_ref, sin_ref)


def add_rows(work_ref, rows_e_ref, rows_o_ref):
    tile, lanes = work_ref.shape[1:]
    odd_x = parity("gx")
    row_e, row_o = start_of(odd_x, tile - HALF, 0), start_of(odd_x, 0, tile - HALF)
    for part in range(2):
        work_ref[part, pl.ds(row_e, HALF)] += rows_e_ref[part, :, :lanes].astype(F32)
        work_ref[part, pl.ds(row_o, HALF)] += rows_o_ref[part, :, :lanes].astype(F32)


def border_kernel(full_ref, rows_e_ref, rows_o_ref, send_e_ref, send_o_ref, work_ref):
    tile = full_ref.shape[1]
    work_ref[...] = full_ref[...]
    add_rows(work_ref, rows_e_ref, rows_o_ref)
    at = tile % 128
    for part in range(2):
        turned = work_ref[part].T
        west = turned[at : at + HALF].astype(BF16)
        east = turned[at + HALF : at + OVER].astype(BF16)

        def store(near, away):
            send_e_ref[part] = near
            send_o_ref[part] = away

        each_way(parity("gy"), lambda: store(east, west), lambda: store(west, east))


def final_kernel(
    full_ref,
    rows_e_ref,
    rows_o_ref,
    cols_e_ref,
    cols_o_ref,
    cos_ref,
    sin_ref,
    result_ref,
    work_ref,
):
    tile = full_ref.shape[1]
    odd_y = parity("gy")
    far = tile - HALF
    lane = lax.broadcasted_iota(jnp.int32, (HALF, tile), 1)
    line = lax.broadcasted_iota(jnp.int32, (HALF, tile), 0)
    pick_e = (lane == line + jnp.where(odd_y == 0, far, 0)).astype(F32).astype(BF16)
    pick_o = (lane == line + jnp.where(odd_y == 0, 0, far)).astype(F32).astype(BF16)

    def outer(values, pick):
        return lax.dot_general(values, pick, (((0,), (0,)), ((), ())), preferred_element_type=F32)

    for part in range(2):
        work_ref[part] = (
            full_ref[part, :, :tile]
            + outer(cols_e_ref[part], pick_e)
            + outer(cols_o_ref[part], pick_o)
        )
    add_rows(work_ref, rows_e_ref, rows_o_ref)
    real, imag = work_ref[0], work_ref[1]
    result_ref[0, 0] = (real * cos_ref[...] - imag * sin_ref[...]).astype(BF16)
    result_ref[1, 0] = (real * sin_ref[...] + imag * cos_ref[...]).astype(BF16)


def phase(freq_ref, slow_ref, cos_ref, sin_ref):
    angle = freq_ref[0] * slow_ref[...]
    turns = jnp.round(angle * (2.0 / math.pi))
    rest = angle - turns * 1.5703125
    rest = rest - turns * 4.8375129699707031e-4
    rest = rest - turns * 7.5495138331e-8
    square = rest * rest
    sine = rest + rest * square * (
        -1.6666654611e-1 + square * (8.3321608736e-3 - square * 1.9515295891e-4)
    )
    cosine = 1.0 - 0.5 * square + square * square * (
        4.166664568298827e-2 + square * (-1.388731625493765e-3 + square * 2.443315711809948e-5)
    )
    quarter = turns.astype(jnp.int32) & 3
    crossed = (quarter & 1) == 1
    sin_value = jnp.where(crossed, cosine, sine)
    cos_value = jnp.where(crossed, sine, cosine)
    sin_ref[...] = jnp.where(quarter >= 2, -sin_value, sin_value)
    cos_ref[...] = jnp.where((quarter == 1) | (quarter == 2), -cos_value, cos_value)


def per_device(
    wavefield, slowness, frequencies, propagator, window_velocity_group, reach_list, coupling
):
    length = propagator.shape[-1]
    span = length - HALF
    wide = 2 * length
    tile_rows, tile_cols = wavefield.shape[2:]
    slots = reach_list.shape[2]

    def shape(*dims, kind=BF16):
        return pltpu.VMEM(dims, kind)

    x_send, rim_send = pl.pallas_call(
        rows_kernel,
        out_shape=(shape(2, span + HALF, tile_cols), shape(2, HALF, tile_cols)),
        in_specs=[VMEM],
        out_specs=(VMEM,) * 2,
        compiler_params=PARAMS,
        cost_estimate=cost(0.5),
        name="rows",
    )(wavefield)
    x_odd = swap(x_send, "gx", True)
    near, far = pl.pallas_call(
        cols_kernel,
        out_shape=(shape(2, tile_rows, span),) * 2,
        in_specs=[VMEM] * 2,
        out_specs=(VMEM,) * 2,
        compiler_params=PARAMS,
        cost_estimate=cost(0.5),
        name="cols",
    )(wavefield, rim_send)
    y_far = swap(far, "gy", True)
    y_near = swap(near, "gy", False)
    rim = swap(rim_send, "gx", False)

    left, right, strip, table = fold(
        propagator,
        cosine_table(length),
        bell_curve(length, OVER),
        reach_list,
        coupling,
        window_velocity_group,
    )

    def call(kernel, name, micros, out_shape, inputs, scratch=(), **options):
        def body(*refs):
            kernel(Lists(refs[0], slots), *refs[1:])

        specs = options.pop("in_specs", [VMEM] * len(inputs))
        outs = options.pop("out_specs", jax.tree.map(lambda _: VMEM, out_shape))
        return pl.pallas_call(
            body,
            out_shape=out_shape,
            in_specs=[SMEM] + specs,
            out_specs=outs,
            scratch_shapes=list(scratch),
            compiler_params=PARAMS,
            name=name,
            cost_estimate=cost(micros),
            **options,
        )(table, *inputs)

    blocks, given = call(
        edge_kernel,
        "edge",
        0.001,
        (shape(4, 4, 2, length, length), shape(2, length, wide)),
        (wavefield, y_near, y_far, left),
        (pltpu.VMEM((4, 2, tile_rows, length), BF16), pltpu.VMEM((2, length, length), F32)),
    )
    got = swap(given, "gx", False)

    def early(c):
        return call(
            functools.partial(early_kernel, c=c),
            "early",
            2,
            (
                shape(2, 2, length, length, kind=F32),
                shape(2, 2, length, slots * OVER),
            ),
            (blocks, left, strip),
        )

    early_e = early(1)
    early_o = early(0)
    x_odd, rim, _ = lax.optimization_barrier((x_odd, rim, given))
    near, far = pl.pallas_call(
        corner_kernel,
        out_shape=(shape(2, span + HALF, span),) * 2,
        in_specs=[VMEM, VMEM],
        out_specs=(VMEM, VMEM),
        compiler_params=PARAMS,
        cost_estimate=cost(0.5),
        name="corner",
    )(x_odd, rim)
    z_far = swap(far, "gy", True)
    z_near = swap(near, "gy", False)
    mid, send_e, send_o = call(
        late_kernel,
        "late",
        4,
        (shape(2, tile_rows, wide, kind=F32), shape(2, HALF, wide), shape(2, HALF, wide)),
        (x_odd, rim, z_near, z_far, left, *early_o, *early_e, right),
        (
            pltpu.VMEM((4, 2, length, length), BF16),
            pltpu.VMEM((2, 4, 2, OVER, length), BF16),
            pltpu.VMEM((2, 2, 2, length, length), F32),
            pltpu.VMEM((2, length, wide), F32),
        ),
    )
    rows_o = swap(send_o, "gx", True)
    rows_e = swap(send_e, "gx", False)

    full, cos_phase, sin_phase = call(
        join_kernel,
        "join",
        3,
        (
            shape(2, tile_rows, wide, kind=F32),
            shape(tile_rows, tile_cols, kind=F32),
            shape(tile_rows, tile_cols, kind=F32),
        ),
        (mid, got, given, right, frequencies, slowness),
        (
            pltpu.VMEM((2, length, wide), F32),
            pltpu.VMEM((2, HALF, wide), F32),
            pltpu.VMEM((tile_rows, tile_cols), F32),
            pltpu.SemaphoreType.DMA((1,)),
        ),
        in_specs=[VMEM] * 4 + [SMEM, HBM],
    )
    last = tile_cols // 128
    side = pl.BlockSpec((2, HALF, 128), lambda i: (0, 0, last))
    send_e, send_o = pl.pallas_call(
        border_kernel,
        grid=(1,),
        out_shape=(shape(2, HALF, tile_rows),) * 2,
        in_specs=[pl.BlockSpec((2, tile_rows, 128), lambda i: (0, 0, last)), side, side],
        out_specs=(pl.BlockSpec((2, HALF, tile_rows), lambda i: (0, 0, 0)),) * 2,
        scratch_shapes=[pltpu.VMEM((2, tile_rows, 128), F32)],
        compiler_params=PARAMS,
        cost_estimate=cost(0.5),
        name="border",
    )(full, rows_e, rows_o)
    cols_o = swap(send_o, "gy", True)
    cols_e = swap(send_e, "gy", False)
    return pl.pallas_call(
        final_kernel,
        out_shape=jax.ShapeDtypeStruct(wavefield.shape, BF16),
        in_specs=[VMEM] * 7,
        out_specs=VMEM,
        scratch_shapes=[pltpu.VMEM((2, tile_rows, tile_cols), F32)],
        compiler_params=PARAMS,
        cost_estimate=cost(1.5),
        name="final",
    )(full, rows_e, rows_o, cols_e, cols_o, cos_phase, sin_phase)


def solution(mesh):
    return jax.shard_map(
        per_device,
        mesh=mesh,
        in_specs=(P(None, None, "gx", "gy"), P("gx", "gy"), P(), P(), P(), P(), P()),
        out_specs=P(None, None, "gx", "gy"),
        check_vma=False,
    )
```

```python
import functools
import math

import jax
import jax.numpy as jnp
import ml_dtypes
import numpy as np
from jax import lax
from jax.experimental import pallas as pl
from jax.experimental.pallas import tpu as pltpu
from jax.sharding import PartitionSpec as P

OVER = 32
HALF = OVER // 2
F32 = jnp.float32
BF16 = jnp.bfloat16
VMEM = pl.BlockSpec(memory_space=pltpu.VMEM)
SMEM = pl.BlockSpec(memory_space=pltpu.SMEM)
ANY = pl.BlockSpec(memory_space=pl.ANY)
PARAMS = pltpu.CompilerParams(vmem_limit_bytes=20 * 2**20)


def cosine_table(length):
    points = np.arange(length, dtype=np.float32) + np.float32(0.5)
    angles = (np.float32(math.pi / length) * points[:, None]) * points[None, :]
    waves = np.cos(angles.astype(np.float64)).astype(np.float32)
    return (np.sqrt(np.float32(2.0 / length)) * waves).astype(ml_dtypes.bfloat16)


def bell_curve(length, margin):
    points = np.arange(length, dtype=np.float64)
    rising = np.sin(0.5 * math.pi * (points + 0.5) / margin)
    falling = np.cos(0.5 * math.pi * (points - (length - margin) + 0.5) / margin)
    bell = np.where(points < margin, rising, np.where(points >= length - margin, falling, 1.0))
    return bell.astype(np.float32)


def dot(left, right):
    return jnp.dot(left, right, preferred_element_type=F32)


def swap(block, axis, odd):
    size = lax.axis_size(axis)
    pairs = []
    for i in range(1 if odd else 0, size - 1, 2):
        pairs += [(i, i + 1), (i + 1, i)]
    return lax.ppermute(block, axis, pairs)


def far_corner(block):
    across, along = (lax.axis_size(axis) for axis in ("gx", "gy"))
    pairs = []
    for x in range(1, across - 1, 2):
        for y in range(1, along - 1, 2):
            first, second = x * along + y, (x + 1) * along + y + 1
            third, fourth = x * along + y + 1, (x + 1) * along + y
            pairs += [(first, second), (second, first), (third, fourth), (fourth, third)]
    return lax.ppermute(block, ("gx", "gy"), pairs)


def parity(axis):
    return lax.rem(lax.axis_index(axis), 2)


def cost(micros):
    return pl.CostEstimate(
        flops=int(micros * 1.1e9), bytes_accessed=int(micros * 3.6e6), transcendentals=0
    )


def fetch(pairs, sems):
    copies = [pltpu.make_async_copy(a, b, sems.at[i]) for i, (a, b) in enumerate(pairs)]
    for copy in copies:
        copy.start()
    return copies


def list_tables(all_reach_ref, all_coup_ref, all_group_ref, table_ref):
    slots, total_y, total_x = all_reach_ref.shape
    odd_x = parity("gx")
    base_x = lax.axis_index("gx") * 2
    base_y = lax.axis_index("gy") * 2
    for row in range(4):
        for col in range(4):
            x = jnp.clip(base_x - 1 + row, 0, total_x - 1)
            y = jnp.clip(base_y - 1 + col, 0, total_y - 1)
            table_ref[row * 4 + col] = all_group_ref[y, x].astype(F32)
    for row in range(3):
        for col in range(2):
            x, y = base_x - odd_x + row, base_y + col
            for slot in range(slots):
                reach = all_reach_ref[slot, y, x]
                place = (lax.div(reach, total_y) - base_x + 1) * 4
                place += lax.rem(reach, total_y) - base_y + 1
                at = 16 + ((row * 2 + col) * slots + slot) * 3
                table_ref[at] = jnp.where(reach >= 0, place, -1).astype(F32)
                table_ref[at + 1] = all_coup_ref[col, slot, 0, x]
                table_ref[at + 2] = all_coup_ref[col, slot, 1, x]


def folded_kernel(
    reach_any,
    coup_any,
    group_any,
    prop_ref,
    cos_ref,
    cos_t_ref,
    row_ref,
    left_ref,
    strip_ref,
    table_any,
    reach_ref,
    coup_ref,
    group_ref,
    table_ref,
    sems,
):
    columns = pl.ds(lax.axis_index("gy") * 2, 2)
    pairs = ((reach_any, reach_ref), (coup_any.at[columns], coup_ref), (group_any, group_ref))
    copies = fetch(pairs, sems)
    out_copy = pltpu.make_async_copy(table_ref, table_any, sems.at[len(copies)])
    groups, _, _, length, _ = prop_ref.shape
    strip_ref[...] = jnp.zeros_like(strip_ref)
    curve = jnp.broadcast_to(row_ref[...], (length, length))
    bell = curve * curve.T
    edge = length - HALF
    for g in range(groups):
        if g == groups - 1:
            for copy in copies:
                copy.wait()
            list_tables(reach_ref, coup_ref, group_ref, table_ref)
            out_copy.start()
        for part in range(2):
            half = dot(prop_ref[g, 0, part], cos_ref[...])
            high = half.astype(BF16)
            low = (half - high.astype(F32)).astype(BF16)
            full = (dot(cos_t_ref[...], high) + dot(cos_t_ref[...], low)) * bell
            left_ref[g, part] = full.astype(BF16)
            strip = jnp.concatenate([full[:, :HALF], full[:, edge:]], axis=1).astype(BF16)
            low = slice(g * OVER, (g + 1) * OVER)
            high = slice(length // 2 + g * OVER, length // 2 + (g + 1) * OVER)
            strip_ref[part, :, low] = strip
            strip_ref[1 - part, :, high] = strip if part == 0 else -strip
    out_copy.wait()

def right_kernel(left_ref, _, right_ref):
    groups, _, length, _ = left_ref.shape
    wide = right_ref.shape[-1]
    inner = wide - 2 * OVER
    edge = length - HALF
    zeros = jnp.zeros((length, wide), BF16)
    for g in range(groups):
        for part in range(2):
            flipped = left_ref[g, part].astype(F32).T.astype(BF16)
            right_ref[g, 0, part] = jnp.concatenate(
                [
                    flipped[:, HALF:],
                    zeros[:, : inner - edge],
                    flipped[:, :HALF],
                    zeros[:, : wide - inner - HALF],
                ],
                axis=1,
            )
            right_ref[g, 1, part] = jnp.concatenate(
                [
                    zeros[:, : inner - edge],
                    flipped[:, :edge],
                    zeros[:, :HALF],
                    flipped[:, edge:],
                    zeros[:, : wide - inner - OVER],
                ],
                axis=1,
            )


def fold(propagator, cosines, bell, reach_list, coupling, window_velocity_group):
    groups, _, _, length, _ = propagator.shape
    slots = reach_list.shape[2]
    entries = 16 + 18 * slots
    return pl.pallas_call(
        folded_kernel,
        out_shape=(
            pltpu.VMEM((groups, 2, length, length), BF16),
            pltpu.VMEM((2, length, length), BF16),
            jax.ShapeDtypeStruct((entries,), F32),
        ),
        in_specs=[ANY] * 3 + [VMEM] * 4,
        out_specs=(VMEM,) * 2 + (ANY,),
        scratch_shapes=[
            pltpu.SMEM(reach_list.shape[::-1], jnp.int32),
            pltpu.SMEM((2, slots, 2, coupling.shape[0]), F32),
            pltpu.SMEM(window_velocity_group.shape[::-1], jnp.int32),
            pltpu.SMEM((entries,), F32),
            pltpu.SemaphoreType.DMA((4,)),
        ],
        compiler_params=PARAMS,
        cost_estimate=cost(0.1),
        name="fold",
    )(
        jnp.transpose(reach_list, (2, 1, 0)),
        jnp.transpose(coupling, (1, 2, 3, 0)),
        window_velocity_group.T,
        propagator,
        cosines,
        cosines.T,
        bell[None, :],
    )


def spread(west, middle, east, part):
    span = west.shape[2]
    wide = middle.shape[2]
    left, centre, right = west[part], middle[part], east[part]
    return (
        jnp.concatenate([left, centre[:, :HALF]], axis=1),
        jnp.concatenate([left[:, span - HALF :], centre[:, :span]], axis=1),
        jnp.concatenate([centre[:, wide - span :], right[:, :HALF]], axis=1),
        jnp.concatenate([centre[:, wide - HALF :], right], axis=1),
    )


def each_way(odd, even_call, odd_call):
    pl.when(odd == 0)(even_call)
    pl.when(odd == 1)(odd_call)


def start_of(odd, if_even, if_odd):
    return pl.multiple_of(jnp.where(odd == 0, if_even, if_odd), HALF)


def sweep(matrix_ref, x_real, x_imag, out_ref):
    t_real, t_imag = matrix_ref[0], matrix_ref[1]
    out_ref[0] = dot(t_real, x_real) - dot(t_imag, x_imag)
    out_ref[1] = dot(t_real, x_imag) + dot(t_imag, x_real)


def mix(base_ref, terms, store):
    length = terms[0][1].shape[1]
    for start in range(0, length, OVER):
        rows = slice(start, start + OVER)
        real, imag = (0.0, 0.0) if base_ref is None else (base_ref[0, rows], base_ref[1, rows])
        for (w_real, w_imag), ref in terms:
            u_real, u_imag = ref[0, rows], ref[1, rows]
            real += w_real * u_real - w_imag * u_imag
            imag += w_real * u_imag + w_imag * u_real
        store(rows, real, imag)


class Lists:
    def __init__(self, table_ref, copy, slots):
        self.table_ref, self.copy, self.slots = table_ref, copy, slots
        self.odd_x = parity("gx")

    def group_at(self, place):
        return self.table_ref[place].astype(jnp.int32)

    def window(self, row, col):
        return (row + 1) * 4 + col + 1

    def entry(self, row, col, slot):
        at = 16 + (((row + self.odd_x) * 2 + col) * self.slots + slot) * 3
        reach = self.table_ref[at].astype(jnp.int32)
        return reach, self.table_ref[at + 1], self.table_ref[at + 2]

    def weight_of(self, row, col, source):
        real, imag = jnp.float32(0), jnp.float32(0)
        for slot in range(self.slots):
            reach, c_real, c_imag = self.entry(row, col, slot)
            real += jnp.where(reach == source, c_real, 0.0)
            imag += jnp.where(reach == source, c_imag, 0.0)
        return real, imag

    def slot_of(self, row, col, slot):
        reach, c_real, c_imag = self.entry(row, col, slot)
        live = reach >= 0
        source = jnp.where(live, reach, self.window(row, col))
        at_row = source // 4
        at_x = jnp.where(self.odd_x == 0, at_row, 3 - at_row)
        real = jnp.where(live, c_real, 0.0)
        imag = jnp.where(live, c_imag, 0.0)
        return self.group_at(source), at_x, source % 4, real, imag


def pack_sides(block, near_ref, far_ref):
    width = near_ref.shape[2]
    start = block.shape[2] - width

    def store(high_ref, low_ref):
        high_ref[...] = block[:, :, start:]
        low_ref[...] = block[:, :, :width]

    each_way(parity("gy"), lambda: store(near_ref, far_ref), lambda: store(far_ref, near_ref))


def rows_kernel(wave_ref, x_ref):
    tile, span = wave_ref.shape[2], x_ref.shape[1]
    for part in range(2):
        x_ref[part] = wave_ref[part, 0, pl.ds(start_of(parity("gx"), 0, tile - span), span)]


def cols_kernel(wave_ref, _, near_ref, far_ref, corner_ref):
    pack_sides(wave_ref.at[:, 0], near_ref, far_ref)
    span = corner_ref.shape[1]
    rows = pl.ds(start_of(parity("gx"), 0, wave_ref.shape[2] - span), span)
    corner_ref[...] = far_ref[:, rows]


def corner_kernel(x_ref, near_ref):
    width = near_ref.shape[2]
    start = x_ref.shape[2] - width
    rows = pl.ds(start_of(parity("gx"), HALF, 0), near_ref.shape[1])

    def store(cols):
        near_ref[...] = x_ref[:, rows, cols]

    each_way(
        parity("gy"), lambda: store(slice(start, start + width)), lambda: store(slice(0, width))
    )


def window_rows(odd_x, at_x, length):
    return pl.multiple_of(jnp.where((at_x == 1) == (odd_x == 0), 0, length - OVER), HALF)


def fill_frame(frame_ref, wave_ref, ye_ref, yo_ref):
    tile = wave_ref.shape[2]
    rim = jnp.zeros((HALF, frame_ref.shape[3]), BF16)

    def fill(west, east):
        for part in range(2):
            for at, block in enumerate(spread(west, wave_ref.at[:, 0], east, part)):
                frame_ref[at, part, HALF : HALF + tile] = block
                frame_ref[at, part, :HALF] = rim
                frame_ref[at, part, HALF + tile :] = rim

    each_way(parity("gy"), lambda: fill(yo_ref, ye_ref), lambda: fill(ye_ref, yo_ref))


def edge_kernel(
    lists, wave_ref, ye_ref, yo_ref, left_ref, frame_ref, part_ref, swept_ref, rim_ref
):
    length = left_ref.shape[-1]
    tile = wave_ref.shape[2]
    fill_frame(frame_ref, wave_ref, ye_ref, yo_ref)
    edge = pl.ds(start_of(lists.odd_x, tile, HALF), HALF)
    for at in range(4):
        for part in range(2):
            rim_ref[at, part] = frame_ref[at, part, edge]
    lists.copy.wait()
    beyond = jnp.where(lists.odd_x == 0, 2, -1)
    mine = jnp.where(lists.odd_x == 0, 1, 0)
    rows = pl.ds(window_rows(lists.odd_x, 2, length), length)
    places = [lists.window(mine, at - 1) for at in range(4)]
    for at, place in enumerate(places):
        matrix_ref = left_ref.at[lists.group_at(place)]
        sweep(matrix_ref, frame_ref[at, 0, rows], frame_ref[at, 1, rows], swept_ref.at[1, at])
    for col in range(2):
        cols = slice(col * length, (col + 1) * length)
        terms = [
            (lists.weight_of(beyond, col, places[at]), swept_ref.at[1, at])
            for at in range(col, col + 3)
        ]

        def store(rows, real, imag):
            part_ref[0, rows, cols] = real.astype(BF16)
            part_ref[1, rows, cols] = imag.astype(BF16)

        mix(None, terms, store)


def early_kernel(
    lists, frame_ref, left_ref, gave_ref, right_ref, _, __, ___, sum_ref, echo_ref, swept_ref
):
    length = left_ref.shape[-1]
    lists.copy.wait()
    beyond = jnp.where(lists.odd_x == 0, 2, -1)
    edge = pl.ds(start_of(lists.odd_x, 0, length - HALF), HALF)
    groups = [lists.group_at(lists.window(beyond, col)) for col in range(2)]
    turn(halves(gave_ref, edge), right_ref, groups, echo_ref)
    rows = pl.ds(window_rows(lists.odd_x, 1, length), length)
    for at in range(4):
        matrix_ref = left_ref.at[lists.group_at(lists.window(lists.odd_x, at - 1))]
        sweep(matrix_ref, frame_ref[at, 0, rows], frame_ref[at, 1, rows], swept_ref.at[0, at])
    for c in range(2):
        for col in range(2):
            terms = []
            for slot in range(lists.slots):
                _, at_x, at_y, w_real, w_imag = lists.slot_of(lists.odd_x ^ c, col, slot)
                inside = (at_x == 1) | (at_x == 2)
                weight = jnp.where(inside, w_real, 0.0), jnp.where(inside, w_imag, 0.0)
                terms.append((weight, swept_ref.at[jnp.clip(at_x - 1, 0, 1), at_y]))

            def store(rows, real, imag):
                sum_ref[c, col, 0, rows] = real
                sum_ref[c, col, 1, rows] = imag

            mix(None, terms, store)


def mix_slots(mixed_ref, groups, weights, pieces):
    half = mixed_ref.shape[0] // 2
    for group, (w_real, w_imag), (real, imag) in zip(groups, weights, pieces):
        real, imag = real.astype(F32), imag.astype(F32)
        at = pl.multiple_of(group * OVER, OVER)
        mixed_ref[pl.ds(at, OVER)] += w_real * real - w_imag * imag
        mixed_ref[pl.ds(half + at, OVER)] += w_real * imag + w_imag * real


def strip_sums(lists, strip_ref, mixed_ref, row, col):
    mixed_ref[...] = jnp.zeros_like(mixed_ref)
    groups, weights, pieces = [], [], []
    for slot in range(lists.slots):
        group, at_x, at_y, w_real, w_imag = lists.slot_of(row, col, slot)
        groups.append(group)
        weights.append((w_real, w_imag))
        pieces.append((strip_ref[at_x, at_y, 0], strip_ref[at_x, at_y, 1]))
    mix_slots(mixed_ref, groups, weights, pieces)
    return mixed_ref[...].astype(BF16)


def late_kernel(
    lists,
    xo_ref,
    rim_ref,
    ze_ref,
    zo_ref,
    left_ref,
    lean_ref,
    frame_ref,
    early_ref,
    right_ref,
    mid_ref,
    rest_ref,
    send_o_ref,
    send_e_ref,
    strip_ref,
    outer_ref,
    swept_ref,
    base_ref,
    mixed_ref,
    sum_ref,
    out_ref,
    border_ref,
):
    length = left_ref.shape[-1]
    span = length - HALF
    tile = mid_ref.shape[1]
    odd_x, odd_y = lists.odd_x, parity("gy")
    at_o, hole_o = start_of(odd_x, 0, HALF), start_of(odd_x, span, 0)
    lean_o, lean_e = start_of(odd_x, 0, HALF), start_of(odd_x, HALF, 0)
    xo_ref = xo_ref.at[:, pl.ds(start_of(odd_x, HALF, 0), span)]
    strip_ref[...] = jnp.zeros_like(strip_ref)

    def fill(west, east):
        for part in range(2):
            for at, block in enumerate(spread(west, xo_ref, east, part)):
                outer_ref[at, part, pl.ds(at_o, span)] = block
                outer_ref[at, part, pl.ds(hole_o, HALF)] = jnp.zeros((HALF, length), BF16)
                strip_ref[2, at, part, pl.ds(lean_e, HALF)] = rim_ref[at, part]

    each_way(odd_y, lambda: fill(zo_ref, ze_ref), lambda: fill(ze_ref, zo_ref))
    shift = start_of(odd_x, span - HALF, HALF)
    near_o, near_e = start_of(odd_x, HALF, tile), start_of(odd_x, tile, HALF)
    for at in range(4):
        for part in range(2):
            strip_ref[1, at, part, pl.ds(lean_o, HALF)] = outer_ref[at, part, pl.ds(shift, HALF)]
            strip_ref[0, at, part, pl.ds(lean_e, HALF)] = frame_ref[at, part, pl.ds(near_o, HALF)]
            strip_ref[3, at, part, pl.ds(lean_o, HALF)] = frame_ref[at, part, pl.ds(near_e, HALF)]

    lists.copy.wait()
    beyond = jnp.where(odd_x == 0, -1, 2)
    places = [lists.window(beyond, at - 1) for at in range(4)]
    for at, place in enumerate(places):
        matrix_ref = left_ref.at[lists.group_at(place)]
        sweep(matrix_ref, outer_ref[at, 0], outer_ref[at, 1], swept_ref.at[at])
    for col in range(2):
        stacked = strip_sums(lists, strip_ref, mixed_ref.at[col], odd_x, col)
        for part in range(2):
            base_ref[part] = early_ref[0, col, part] + dot(lean_ref[part], stacked)
        cols = slice(col * length, (col + 1) * length)
        terms = [
            (lists.weight_of(odd_x, col, places[at]), swept_ref.at[at])
            for at in range(col, col + 3)
        ]

        def store(rows, real, imag):
            sum_ref[0, rows, cols] = real.astype(BF16)
            sum_ref[1, rows, cols] = imag.astype(BF16)

        mix(base_ref, terms, store)
    groups = [lists.group_at(lists.window(odd_x, col)) for col in range(2)]
    turn(halves(sum_ref, slice(None)), right_ref, groups, out_ref)
    source = start_of(odd_x, HALF, 0)
    target = start_of(odd_x, 0, tile - span)
    border = start_of(odd_x, 0, span)
    for part in range(2):
        mid_ref[part, pl.ds(target, span)] = out_ref[part, pl.ds(source, span)]
        send_o_ref[part] = out_ref[part, pl.ds(border, HALF)].astype(BF16)
    row = 1 - odd_x
    for col in range(2):
        stacked = strip_sums(lists, strip_ref, mixed_ref.at[2 + col], row, col)
        for part in range(2):
            rest_ref[part, :, col * length : (col + 1) * length] = early_ref[1, col, part] + dot(
                lean_ref[part], stacked
            )
    groups = [lists.group_at(lists.window(row, col)) for col in range(2)]
    rows = pl.ds(start_of(odd_x, span, 0), HALF)
    turn(halves(rest_ref, rows), right_ref, groups, border_ref)
    for part in range(2):
        send_e_ref[part] = border_ref[part, :, : send_e_ref.shape[2]].astype(BF16)


def halves(ref, rows):
    length = ref.shape[2] // 2
    return [
        [ref[part, rows, col * length : (col + 1) * length].astype(BF16) for part in range(2)]
        for col in range(2)
    ]


def turn(blocks, right_ref, groups, out_ref):
    real, imag = 0.0, 0.0
    for col in range(2):
        m_real, m_imag = blocks[col]
        r_real, r_imag = right_ref[groups[col], col, 0], right_ref[groups[col], col, 1]
        real += dot(m_real, r_real) - dot(m_imag, r_imag)
        imag += dot(m_real, r_imag) + dot(m_imag, r_real)
    out_ref[0] = real
    out_ref[1] = imag


def join_kernel(lists, mid_ref, rest_ref, got_ref, right_ref, full_ref, sum_ref, out_ref):
    length = got_ref.shape[1]
    span = length - HALF
    tile = full_ref.shape[1]
    odd_x = lists.odd_x
    mine = jnp.where(odd_x == 0, 1, 0)
    for part in range(2):
        sum_ref[part] = (rest_ref[part] + got_ref[part].astype(F32)).astype(BF16)
    lists.copy.wait()
    groups = [lists.group_at(lists.window(mine, col)) for col in range(2)]
    turn(halves(sum_ref, slice(None)), right_ref, groups, out_ref)
    alone = tile - span
    both = slice(alone, span)
    source, target = start_of(odd_x, span - alone, HALF), start_of(odd_x, span, 0)
    shared = start_of(odd_x, 0, HALF + alone)
    for part in range(2):
        full_ref[part, pl.ds(target, alone)] = out_ref[part, pl.ds(source, alone)]
        full_ref[part, both] = (
            mid_ref[part, both] + out_ref[part, pl.ds(shared, span - alone)]
        )


def border_kernel(full_ref, echo_ref, rows_e_ref, rows_o_ref, done_ref, send_e_ref, send_o_ref):
    tile = done_ref.shape[1]
    lanes = tile // 128 * 128
    odd_x = parity("gx")
    row_e = pl.ds(start_of(odd_x, tile - HALF, 0), HALF)
    row_o = pl.ds(start_of(odd_x, 0, tile - HALF), HALF)
    width = rows_e_ref.shape[2]
    for part in range(2):
        done_ref[part, row_o] = full_ref[part, row_o] + rows_o_ref[part].astype(F32)
        done_ref[part, row_e, :width] = (
            full_ref[part, row_e, :width]
            + echo_ref[part, :, :width]
            + rows_e_ref[part].astype(F32)
        )
        turned = done_ref[part, :, lanes:].T
        west = turned[tile - lanes : tile - lanes + HALF].astype(BF16)
        east = turned[tile - lanes + HALF : tile - lanes + OVER].astype(BF16)

        def store(near, away):
            send_e_ref[part] = near
            send_o_ref[part] = away

        each_way(parity("gy"), lambda: store(east, west), lambda: store(west, east))


def rotate(real, imag, cos, sin, result_ref):
    result_ref[0, 0] = (real * cos - imag * sin).astype(BF16)
    result_ref[1, 0] = (real * sin + imag * cos).astype(BF16)


def inner_kernel(full_ref, cos_ref, sin_ref, result_ref):
    rotate(full_ref[0], full_ref[1], cos_ref[...], sin_ref[...], result_ref)


def outer_kernel(
    _, full_ref, cols_e_ref, cols_o_ref, cos_ref, sin_ref, result_hbm, west_ref, east_ref, sems
):
    tile = full_ref.shape[1]
    lanes = tile // 128 * 128

    def side(cols_ref, cols, shift, out_ref):
        size = cols.stop - cols.start
        lane = lax.broadcasted_iota(jnp.int32, (HALF, size), 1)
        line = lax.broadcasted_iota(jnp.int32, (HALF, size), 0)
        pick = (lane == line + shift).astype(F32).astype(BF16)
        real, imag = (
            full_ref[part, :, cols]
            + lax.dot_general(
                cols_ref[part], pick, (((0,), (0,)), ((), ())), preferred_element_type=F32
            )
            for part in range(2)
        )
        rotate(real, imag, cos_ref[:, cols], sin_ref[:, cols], out_ref)

    west, east = slice(0, 128), slice(lanes, tile)
    copies = [
        pltpu.make_async_copy(ref, result_hbm.at[:, :, :, cols], sems.at[i])
        for i, (ref, cols) in enumerate(((west_ref, west), (east_ref, east)))
    ]

    def sides(to_west_ref, to_east_ref):
        side(to_west_ref, west, 0, west_ref)
        copies[0].start()
        side(to_east_ref, east, tile - HALF - lanes, east_ref)
        copies[1].start()

    each_way(
        parity("gy"), lambda: sides(cols_o_ref, cols_e_ref), lambda: sides(cols_e_ref, cols_o_ref)
    )
    for copy in copies:
        copy.wait()


def phase_kernel(freq_ref, slow_ref, _, cos_ref, sin_ref):
    angle = freq_ref[...] * slow_ref[...]
    turns = jnp.round(angle * (2.0 / math.pi))
    rest = angle - turns * 1.5703125
    rest = rest - turns * 4.8375129699707031e-4
    rest = rest - turns * 7.5495138331e-8
    square = rest * rest
    sine = rest + rest * square * (
        -1.6666654611e-1 + square * (8.3321608736e-3 - square * 1.9515295891e-4)
    )
    cosine = 1.0 - 0.5 * square + square * square * (
        4.166664568298827e-2 + square * (-1.388731625493765e-3 + square * 2.443315711809948e-5)
    )
    quarter = turns.astype(jnp.int32) & 3
    crossed = (quarter & 1) == 1
    sin_value = jnp.where(crossed, cosine, sine)
    cos_value = jnp.where(crossed, sine, cosine)
    sin_ref[...] = jnp.where(quarter >= 2, -sin_value, sin_value)
    cos_ref[...] = jnp.where((quarter == 1) | (quarter == 2), -cos_value, cos_value)


def per_device(
    wavefield, slowness, frequencies, propagator, window_velocity_group, reach_list, coupling
):
    length = propagator.shape[-1]
    span = length - HALF
    wide = 2 * length
    tile_rows, tile_cols = wavefield.shape[2:]
    slots = reach_list.shape[2]

    def shape(*dims, kind=BF16):
        return pltpu.VMEM(dims, kind)

    x_send = pl.pallas_call(
        rows_kernel,
        out_shape=shape(2, span + HALF, tile_cols),
        in_specs=[VMEM],
        out_specs=VMEM,
        compiler_params=PARAMS,
        cost_estimate=cost(0.5),
        name="rows",
    )(wavefield)
    x_odd = swap(x_send, "gx", True)
    near, far, corner = pl.pallas_call(
        cols_kernel,
        out_shape=(shape(2, tile_rows, span),) * 2 + (shape(2, span, span),),
        in_specs=[VMEM] * 2,
        out_specs=(VMEM,) * 3,
        compiler_params=PARAMS,
        cost_estimate=cost(0.5),
        name="cols",
    )(wavefield, x_send)
    y_near = swap(near, "gy", False)
    y_far = swap(far, "gy", True)
    z_far = far_corner(corner)
    y_near = swap(near, "gy", False)

    left, strip, table = fold(
        propagator,
        cosine_table(length),
        bell_curve(length, OVER),
        reach_list,
        coupling,
        window_velocity_group,
    )
    def call(kernel, name, micros, out_shape, inputs, scratch=(), **options):
        def body(table_any, *refs):
            *refs, table_ref, sem = refs
            copy = pltpu.make_async_copy(table_any, table_ref, sem)
            copy.start()
            kernel(Lists(table_ref, copy, slots), *refs)

        specs = options.pop("in_specs", [VMEM] * len(inputs))
        outs = options.pop("out_specs", jax.tree.map(lambda _: VMEM, out_shape))
        return pl.pallas_call(
            body,
            out_shape=out_shape,
            in_specs=[ANY] + specs,
            out_specs=outs,
            scratch_shapes=list(scratch)
            + [pltpu.SMEM(table.shape, F32), pltpu.SemaphoreType.DMA(())],
            compiler_params=PARAMS,
            name=name,
            cost_estimate=cost(micros),
            **options,
        )(table, *inputs)

    frame, given, swept, rim_send = call(
        edge_kernel,
        "edge",
        0.001,
        (
            shape(4, 2, tile_rows + OVER, length),
            shape(2, length, wide),
            shape(2, 4, 2, length, length, kind=F32),
            shape(4, 2, HALF, length),
        ),
        (wavefield, y_near, y_far, left),
    )
    rim = swap(rim_send, "gx", False)
    got = swap(given, "gx", False)

    right = pl.pallas_call(
        right_kernel,
        out_shape=shape(left.shape[0], 2, 2, length, wide),
        in_specs=[VMEM, ANY],
        out_specs=VMEM,
        compiler_params=PARAMS,
        cost_estimate=cost(0.01),
        name="right",
    )(left, rim_send)
    cos_phase, sin_phase = pl.pallas_call(
        phase_kernel,
        out_shape=(shape(tile_rows, tile_cols, kind=F32),) * 2,
        in_specs=[VMEM] * 2 + [ANY],
        out_specs=(VMEM,) * 2,
        compiler_params=PARAMS,
        cost_estimate=cost(0.01),
        name="phase",
    )(jnp.broadcast_to(frequencies[:, None], (1, tile_cols)), slowness, rim_send)

    early, echo, _ = call(
        early_kernel,
        "early",
        3,
        (
            shape(2, 2, 2, length, length, kind=F32),
            shape(2, HALF, wide, kind=F32),
            shape(2, 4, 2, length, length, kind=F32),
        ),
        (frame, left, given, right, swept, z_far, cos_phase),
        in_specs=[VMEM] * 5 + [ANY] * 2,
        input_output_aliases={5: 2},
    )
    near = pl.pallas_call(
        corner_kernel,
        out_shape=shape(2, span, span),
        in_specs=[VMEM],
        out_specs=VMEM,
        compiler_params=PARAMS,
        cost_estimate=cost(0.2),
        name="corner",
    )(x_odd)
    z_near = swap(near, "gy", False)
    mid, rest, send_o, send_e = call(
        late_kernel,
        "late",
        4,
        (
            shape(2, tile_rows, wide, kind=F32),
            shape(2, length, wide, kind=F32),
            shape(2, HALF, wide),
            shape(2, HALF, tile_cols + OVER),
        ),
        (x_odd, rim, z_near, z_far, left, strip, frame, early, right),
        (
            pltpu.VMEM((4, 4, 2, OVER, length), BF16),
            pltpu.VMEM((4, 2, length, length), BF16),
            pltpu.VMEM((4, 2, length, length), F32),
            pltpu.VMEM((2, length, length), F32),
            pltpu.VMEM((4, length, length), F32),
            pltpu.VMEM((2, length, wide), BF16),
            pltpu.VMEM((2, length, wide), F32),
            pltpu.VMEM((2, HALF, wide), F32),
        ),
    )
    rows_o = swap(send_o, "gx", True)
    rows_e = swap(send_e, "gx", False)
    full = call(
        join_kernel,
        "join",
        0.001,
        shape(2, tile_rows, wide, kind=F32),
        (mid, rest, got, right),
        (
            pltpu.VMEM((2, length, wide), BF16),
            pltpu.VMEM((2, length, wide), F32),
        ),
        input_output_aliases={1: 0},
    )
    full, send_e, send_o = pl.pallas_call(
        border_kernel,
        out_shape=(shape(2, tile_rows, wide, kind=F32),) + (shape(2, HALF, tile_rows),) * 2,
        in_specs=[VMEM] * 4,
        out_specs=(VMEM,) * 3,
        input_output_aliases={0: 0},
        compiler_params=PARAMS,
        cost_estimate=cost(0.5),
        name="border",
    )(full, echo, rows_e, rows_o)
    cols_o = swap(send_o, "gy", True)
    cols_e = swap(send_e, "gy", False)
    result = jax.ShapeDtypeStruct(wavefield.shape, BF16)
    count = -(-tile_cols // 128)

    def blocks(place):
        return (
            pl.BlockSpec((2, tile_rows, 128), lambda i: (0, 0, place(i))),
            pl.BlockSpec((tile_rows, 128), lambda i: (0, place(i))),
            pl.BlockSpec((2, 1, tile_rows, 128), lambda i: (0, 0, 0, place(i))),
        )

    full_spec, phase_spec, out_spec = blocks(lambda i: i + 1)
    partly = pl.pallas_call(
        inner_kernel,
        grid=(count - 2,),
        out_shape=result,
        in_specs=[full_spec, phase_spec, phase_spec],
        out_specs=out_spec,
        compiler_params=PARAMS,
        cost_estimate=cost(1),
        name="inner",
    )(full, cos_phase, sin_phase)
    return pl.pallas_call(
        outer_kernel,
        out_shape=result,
        in_specs=[ANY] + [VMEM] * 5,
        out_specs=ANY,
        scratch_shapes=[
            pltpu.VMEM((2, 1, tile_rows, 128), BF16),
            pltpu.VMEM((2, 1, tile_rows, tile_cols % 128), BF16),
            pltpu.SemaphoreType.DMA((2,)),
        ],
        input_output_aliases={0: 0},
        compiler_params=PARAMS,
        cost_estimate=cost(1),
        name="outer",
    )(partly, full, cols_e, cols_o, cos_phase, sin_phase)


def solution(mesh):
    return jax.shard_map(
        per_device,
        mesh=mesh,
        in_specs=(P(None, None, "gx", "gy"), P("gx", "gy"), P(), P(), P(), P(), P()),
        out_specs=P(None, None, "gx", "gy"),
        check_vma=False,
    )
```

```python
import functools
import math

import jax
import jax.numpy as jnp
import ml_dtypes
import numpy as np
from jax import lax
from jax.experimental import pallas as pl
from jax.experimental.pallas import tpu as pltpu
from jax.sharding import PartitionSpec as P

OVER = 32
HALF = OVER // 2
F32 = jnp.float32
BF16 = jnp.bfloat16
VMEM = pl.BlockSpec(memory_space=pltpu.VMEM)
SMEM = pl.BlockSpec(memory_space=pltpu.SMEM)
ANY = pl.BlockSpec(memory_space=pl.ANY)
PARAMS = pltpu.CompilerParams(vmem_limit_bytes=20 * 2**20)


def cosine_table(length):
    points = np.arange(length, dtype=np.float32) + np.float32(0.5)
    angles = (np.float32(math.pi / length) * points[:, None]) * points[None, :]
    waves = np.cos(angles.astype(np.float64)).astype(np.float32)
    return (np.sqrt(np.float32(2.0 / length)) * waves).astype(ml_dtypes.bfloat16)


def bell_curve(length, margin):
    points = np.arange(length, dtype=np.float64)
    rising = np.sin(0.5 * math.pi * (points + 0.5) / margin)
    falling = np.cos(0.5 * math.pi * (points - (length - margin) + 0.5) / margin)
    bell = np.where(points < margin, rising, np.where(points >= length - margin, falling, 1.0))
    return bell.astype(np.float32)


def dot(left, right):
    return jnp.dot(left, right, preferred_element_type=F32)


def swap(block, axis, odd):
    size = lax.axis_size(axis)
    pairs = []
    for i in range(1 if odd else 0, size - 1, 2):
        pairs += [(i, i + 1), (i + 1, i)]
    return lax.ppermute(block, axis, pairs)


def far_corner(block):
    across, along = (lax.axis_size(axis) for axis in ("gx", "gy"))
    pairs = []
    for x in range(1, across - 1, 2):
        for y in range(1, along - 1, 2):
            first, second = x * along + y, (x + 1) * along + y + 1
            third, fourth = x * along + y + 1, (x + 1) * along + y
            pairs += [(first, second), (second, first), (third, fourth), (fourth, third)]
    return lax.ppermute(block, ("gx", "gy"), pairs)


def parity(axis):
    return lax.rem(lax.axis_index(axis), 2)


def cost(micros):
    return pl.CostEstimate(
        flops=int(micros * 1.1e9), bytes_accessed=int(micros * 3.6e6), transcendentals=0
    )


def fetch(pairs, sems):
    copies = [pltpu.make_async_copy(a, b, sems.at[i]) for i, (a, b) in enumerate(pairs)]
    for copy in copies:
        copy.start()
    return copies


def list_tables(all_reach_ref, all_coup_ref, all_group_ref, place_ref, weight_ref):
    slots, total_y, total_x = all_reach_ref.shape
    odd_x = parity("gx")
    base_x = lax.axis_index("gx") * 2
    base_y = lax.axis_index("gy") * 2
    for row in range(4):
        for col in range(4):
            x = jnp.clip(base_x - 1 + row, 0, total_x - 1)
            y = jnp.clip(base_y - 1 + col, 0, total_y - 1)
            place_ref[row * 4 + col] = all_group_ref[y, x]
    for row in range(3):
        for col in range(2):
            x, y = base_x - odd_x + row, base_y + col
            here = (row - odd_x + 1) * 4 + col + 1
            for slot in range(slots):
                reach = all_reach_ref[slot, y, x]
                step = reach - (x * total_y + y)
                down = jnp.where(step > 1, 1, jnp.where(step < -1, -1, 0))
                place = here + step + down * (4 - total_y)
                at = (row * 2 + col) * slots + slot
                place_ref[16 + at] = jnp.where(reach >= 0, place, -1)
                weight_ref[at * 2] = all_coup_ref[col, slot, 0, x]
                weight_ref[at * 2 + 1] = all_coup_ref[col, slot, 1, x]


def folded_kernel(
    reach_any,
    coup_any,
    group_any,
    prop_ref,
    cos_ref,
    cos_t_ref,
    row_ref,
    left_ref,
    strip_ref,
    place_any,
    weight_any,
    reach_ref,
    coup_ref,
    group_ref,
    place_ref,
    weight_ref,
    sems,
):
    columns = pl.ds(lax.axis_index("gy") * 2, 2)
    pairs = ((reach_any, reach_ref), (coup_any.at[columns], coup_ref), (group_any, group_ref))
    copies = fetch(pairs, sems)
    groups, _, _, length, _ = prop_ref.shape
    strip_ref[...] = jnp.zeros_like(strip_ref)
    curve = jnp.broadcast_to(row_ref[...], (length, length))
    bell = curve * curve.T
    edge = length - HALF
    for g in range(groups):
        if g == groups - 1:
            for copy in copies:
                copy.wait()
            list_tables(reach_ref, coup_ref, group_ref, place_ref, weight_ref)
            outward = fetch(((place_ref, place_any), (weight_ref, weight_any)), sems.at[3:])
        for part in range(2):
            half = dot(prop_ref[g, 0, part], cos_ref[...])
            high = half.astype(BF16)
            low = (half - high.astype(F32)).astype(BF16)
            full = (dot(cos_t_ref[...], high) + dot(cos_t_ref[...], low)) * bell
            left_ref[g, part] = full.astype(BF16)
            strip = jnp.concatenate([full[:, :HALF], full[:, edge:]], axis=1).astype(BF16)
            low = slice(g * OVER, (g + 1) * OVER)
            high = slice(length // 2 + g * OVER, length // 2 + (g + 1) * OVER)
            strip_ref[part, :, low] = strip
            strip_ref[1 - part, :, high] = strip if part == 0 else -strip
    for copy in outward:
        copy.wait()

def right_kernel(left_ref, right_ref):
    groups, _, length, _ = left_ref.shape
    wide = right_ref.shape[-1]
    inner = wide - 2 * OVER
    edge = length - HALF
    zeros = jnp.zeros((length, wide), BF16)
    for g in range(groups):
        for part in range(2):
            flipped = left_ref[g, part].astype(F32).T.astype(BF16)
            right_ref[g, 0, part] = jnp.concatenate(
                [
                    flipped[:, HALF:],
                    zeros[:, : inner - edge],
                    flipped[:, :HALF],
                    zeros[:, : wide - inner - HALF],
                ],
                axis=1,
            )
            right_ref[g, 1, part] = jnp.concatenate(
                [
                    zeros[:, : inner - edge],
                    flipped[:, :edge],
                    zeros[:, :HALF],
                    flipped[:, edge:],
                    zeros[:, : wide - inner - OVER],
                ],
                axis=1,
            )


def fold(propagator, cosines, bell, reach_list, coupling, window_velocity_group):
    groups, _, _, length, _ = propagator.shape
    slots = reach_list.shape[2]
    entries = 6 * slots
    return pl.pallas_call(
        folded_kernel,
        out_shape=(
            pltpu.VMEM((groups, 2, length, length), BF16),
            pltpu.VMEM((2, length, length), BF16),
            jax.ShapeDtypeStruct((16 + entries,), jnp.int32),
            jax.ShapeDtypeStruct((2 * entries,), F32),
        ),
        in_specs=[ANY] * 3 + [VMEM] * 4,
        out_specs=(VMEM,) * 2 + (ANY,) * 2,
        scratch_shapes=[
            pltpu.SMEM(reach_list.shape[::-1], jnp.int32),
            pltpu.SMEM((2, slots, 2, coupling.shape[0]), F32),
            pltpu.SMEM(window_velocity_group.shape[::-1], jnp.int32),
            pltpu.SMEM((16 + entries,), jnp.int32),
            pltpu.SMEM((2 * entries,), F32),
            pltpu.SemaphoreType.DMA((5,)),
        ],
        compiler_params=PARAMS,
        cost_estimate=cost(0.1),
        name="fold",
    )(
        jnp.transpose(reach_list, (2, 1, 0)),
        jnp.transpose(coupling, (1, 2, 3, 0)),
        window_velocity_group.T,
        propagator,
        cosines,
        cosines.T,
        bell[None, :],
    )


def spread(west, middle, east, part):
    span = west.shape[2]
    wide = 2 * (span - HALF)
    left, centre, right = west[part], middle[part], east[part]
    return (
        jnp.concatenate([left, centre[:, :HALF]], axis=1),
        jnp.concatenate([left[:, span - HALF :], centre[:, :span]], axis=1),
        jnp.concatenate([centre[:, wide - span : wide], right[:, :HALF]], axis=1),
        jnp.concatenate([centre[:, wide - HALF : wide], right], axis=1),
    )


def each_way(odd, even_call, odd_call):
    pl.when(odd == 0)(even_call)
    pl.when(odd == 1)(odd_call)


def start_of(odd, if_even, if_odd):
    return pl.multiple_of(jnp.where(odd == 0, if_even, if_odd), HALF)


def sweep(matrix_ref, x_real, x_imag, out_ref):
    t_real, t_imag = matrix_ref[0], matrix_ref[1]
    out_ref[0] = dot(t_real, x_real) - dot(t_imag, x_imag)
    out_ref[1] = dot(t_real, x_imag) + dot(t_imag, x_real)


def mix(base_ref, terms, store):
    length = terms[0][1].shape[1]
    for start in range(0, length, OVER):
        rows = slice(start, start + OVER)
        real, imag = (0.0, 0.0) if base_ref is None else (base_ref[0, rows], base_ref[1, rows])
        for (w_real, w_imag), ref in terms:
            u_real, u_imag = ref[0, rows], ref[1, rows]
            real += w_real * u_real - w_imag * u_imag
            imag += w_real * u_imag + w_imag * u_real
        store(rows, real, imag)


class Lists:
    def __init__(self, place_ref, weight_ref, copies, slots):
        self.place_ref, self.weight_ref = place_ref, weight_ref
        self.copies, self.slots = copies, slots
        self.odd_x = parity("gx")

    def wait(self):
        for copy in self.copies:
            copy.wait()

    def group_at(self, place):
        return self.place_ref[place]

    def window(self, row, col):
        return (row + 1) * 4 + col + 1

    def entry(self, row, col, slot):
        at = ((row + self.odd_x) * 2 + col) * self.slots + slot
        return self.place_ref[16 + at], self.weight_ref[at * 2], self.weight_ref[at * 2 + 1]

    def weight_of(self, row, col, source):
        real, imag = jnp.float32(0), jnp.float32(0)
        for slot in range(self.slots):
            reach, c_real, c_imag = self.entry(row, col, slot)
            real += jnp.where(reach == source, c_real, 0.0)
            imag += jnp.where(reach == source, c_imag, 0.0)
        return real, imag

    def slot_of(self, row, col, slot):
        reach, c_real, c_imag = self.entry(row, col, slot)
        live = reach >= 0
        source = jnp.where(live, reach, self.window(row, col))
        at_row = source >> 2
        at_x = jnp.where(self.odd_x == 0, at_row, 3 - at_row)
        real = jnp.where(live, c_real, 0.0)
        imag = jnp.where(live, c_imag, 0.0)
        return self.group_at(source), at_x, source & 3, real, imag


def pack_sides(block, near_ref, far_ref):
    width = near_ref.shape[2]
    start = block.shape[2] - width

    def store(high_ref, low_ref):
        high_ref[...] = block[:, :, start:]
        low_ref[...] = block[:, :, :width]

    each_way(parity("gy"), lambda: store(near_ref, far_ref), lambda: store(far_ref, near_ref))


def rows_kernel(wave_ref, x_ref):
    tile, span = wave_ref.shape[2], x_ref.shape[1]
    for part in range(2):
        rows = pl.ds(start_of(parity("gx"), 0, tile - span), span)
        x_ref[part, :, :tile] = wave_ref[part, 0, rows]
        x_ref[part, :, tile:] = jnp.zeros((span, x_ref.shape[2] - tile), BF16)


def cols_kernel(wave_ref, _, near_ref, far_ref, corner_ref):
    pack_sides(wave_ref.at[:, 0], near_ref, far_ref)
    span = corner_ref.shape[1]
    rows = pl.ds(start_of(parity("gx"), 0, wave_ref.shape[2] - span), span)
    corner_ref[...] = far_ref[:, rows]


def corner_kernel(x_ref, _, near_ref):
    width = near_ref.shape[2]
    start = 2 * (width - HALF) - width

    def store(cols):
        near_ref[...] = x_ref[:, :, cols]

    each_way(
        parity("gy"), lambda: store(slice(start, start + width)), lambda: store(slice(0, width))
    )


def window_rows(odd_x, at_x, length):
    return pl.multiple_of(jnp.where((at_x == 1) == (odd_x == 0), 0, length - OVER), HALF)


def fill_frame(frame_ref, wave_ref, ye_ref, yo_ref):
    tile = wave_ref.shape[2]
    rim = jnp.zeros((HALF, frame_ref.shape[3]), BF16)

    def fill(west, east):
        for part in range(2):
            for at, block in enumerate(spread(west, wave_ref.at[:, 0], east, part)):
                frame_ref[at, part, HALF : HALF + tile] = block
                frame_ref[at, part, :HALF] = rim
                frame_ref[at, part, HALF + tile :] = rim

    each_way(parity("gy"), lambda: fill(yo_ref, ye_ref), lambda: fill(ye_ref, yo_ref))


def edge_kernel(
    lists,
    wave_ref,
    ye_ref,
    yo_ref,
    left_ref,
    _,
    frame_ref,
    send_ref,
    border_ref,
    swept_ref,
    rim_ref,
    part_ref,
):
    length = left_ref.shape[-1]
    tile = wave_ref.shape[2]
    fill_frame(frame_ref, wave_ref, ye_ref, yo_ref)
    edge = pl.ds(start_of(lists.odd_x, tile, HALF), HALF)
    for at in range(4):
        for part in range(2):
            rim_ref[at, part] = frame_ref[at, part, edge]
    lists.wait()
    beyond = jnp.where(lists.odd_x == 0, 2, -1)
    mine = jnp.where(lists.odd_x == 0, 1, 0)
    rows = pl.ds(window_rows(lists.odd_x, 2, length), length)
    places = [lists.window(mine, at - 1) for at in range(4)]
    for at, place in enumerate(places):
        matrix_ref = left_ref.at[lists.group_at(place)]
        sweep(matrix_ref, frame_ref[at, 0, rows], frame_ref[at, 1, rows], swept_ref.at[1, at])
    for col in range(2):
        cols = slice(col * length, (col + 1) * length)
        terms = [
            (lists.weight_of(beyond, col, places[at]), swept_ref.at[1, at])
            for at in range(col, col + 3)
        ]

        def store(rows, real, imag):
            part_ref[0, rows, cols] = real.astype(BF16)
            part_ref[1, rows, cols] = imag.astype(BF16)

        mix(None, terms, store)
    span = length - HALF
    inner, outer = start_of(lists.odd_x, HALF, 0), start_of(lists.odd_x, 0, span)
    for part in range(2):
        send_ref[part] = part_ref[part, pl.ds(inner, span)]
        border_ref[part] = part_ref[part, pl.ds(outer, HALF)]


def early_kernel(
    lists, frame_ref, left_ref, gave_ref, right_ref, _, sum_ref, echo_ref, swept_ref
):
    length = left_ref.shape[-1]
    lists.wait()
    beyond = jnp.where(lists.odd_x == 0, 2, -1)
    groups = [lists.group_at(lists.window(beyond, col)) for col in range(2)]
    turn(halves(gave_ref, slice(None)), right_ref, groups, echo_ref)
    rows = pl.ds(window_rows(lists.odd_x, 1, length), length)
    for at in range(4):
        matrix_ref = left_ref.at[lists.group_at(lists.window(lists.odd_x, at - 1))]
        sweep(matrix_ref, frame_ref[at, 0, rows], frame_ref[at, 1, rows], swept_ref.at[0, at])
    for c in range(2):
        for col in range(2):
            terms = []
            for slot in range(lists.slots):
                _, at_x, at_y, w_real, w_imag = lists.slot_of(lists.odd_x ^ c, col, slot)
                inside = (at_x == 1) | (at_x == 2)
                weight = jnp.where(inside, w_real, 0.0), jnp.where(inside, w_imag, 0.0)
                terms.append((weight, swept_ref.at[jnp.clip(at_x - 1, 0, 1), at_y]))

            def store(rows, real, imag):
                sum_ref[c, col, 0, rows] = real
                sum_ref[c, col, 1, rows] = imag

            mix(None, terms, store)


def mix_slots(mixed_ref, groups, weights, pieces):
    half = mixed_ref.shape[0] // 2
    for group, (w_real, w_imag), (real, imag) in zip(groups, weights, pieces):
        real, imag = real.astype(F32), imag.astype(F32)
        at = pl.multiple_of(group * OVER, OVER)
        mixed_ref[pl.ds(at, OVER)] += w_real * real - w_imag * imag
        mixed_ref[pl.ds(half + at, OVER)] += w_real * imag + w_imag * real


def strip_sums(lists, strip_ref, mixed_ref, row, col):
    mixed_ref[...] = jnp.zeros_like(mixed_ref)
    groups, weights, pieces = [], [], []
    for slot in range(lists.slots):
        group, at_x, at_y, w_real, w_imag = lists.slot_of(row, col, slot)
        groups.append(group)
        weights.append((w_real, w_imag))
        pieces.append((strip_ref[at_x, at_y, 0], strip_ref[at_x, at_y, 1]))
    mix_slots(mixed_ref, groups, weights, pieces)
    return mixed_ref[...].astype(BF16)


def late_kernel(
    lists,
    xo_ref,
    rim_ref,
    ze_ref,
    zo_ref,
    left_ref,
    lean_ref,
    frame_ref,
    early_ref,
    right_ref,
    mid_ref,
    rest_ref,
    send_o_ref,
    send_e_ref,
    strip_ref,
    outer_ref,
    swept_ref,
    base_ref,
    mixed_ref,
    sum_ref,
    out_ref,
    border_ref,
):
    length = left_ref.shape[-1]
    span = length - HALF
    tile = mid_ref.shape[1]
    odd_x, odd_y = lists.odd_x, parity("gy")
    at_o, hole_o = start_of(odd_x, 0, HALF), start_of(odd_x, span, 0)
    lean_o, lean_e = start_of(odd_x, 0, HALF), start_of(odd_x, HALF, 0)
    strip_ref[...] = jnp.zeros_like(strip_ref)

    def fill(west, east):
        for part in range(2):
            for at, block in enumerate(spread(west, xo_ref, east, part)):
                outer_ref[at, part, pl.ds(at_o, span)] = block
                outer_ref[at, part, pl.ds(hole_o, HALF)] = jnp.zeros((HALF, length), BF16)
                strip_ref[2, at, part, pl.ds(lean_e, HALF)] = rim_ref[at, part]

    each_way(odd_y, lambda: fill(zo_ref, ze_ref), lambda: fill(ze_ref, zo_ref))
    shift = start_of(odd_x, span - HALF, HALF)
    near_o, near_e = start_of(odd_x, HALF, tile), start_of(odd_x, tile, HALF)
    for at in range(4):
        for part in range(2):
            strip_ref[1, at, part, pl.ds(lean_o, HALF)] = outer_ref[at, part, pl.ds(shift, HALF)]
            strip_ref[0, at, part, pl.ds(lean_e, HALF)] = frame_ref[at, part, pl.ds(near_o, HALF)]
            strip_ref[3, at, part, pl.ds(lean_o, HALF)] = frame_ref[at, part, pl.ds(near_e, HALF)]

    lists.wait()
    beyond = jnp.where(odd_x == 0, -1, 2)
    places = [lists.window(beyond, at - 1) for at in range(4)]
    for at, place in enumerate(places):
        matrix_ref = left_ref.at[lists.group_at(place)]
        sweep(matrix_ref, outer_ref[at, 0], outer_ref[at, 1], swept_ref.at[at])
    for col in range(2):
        stacked = strip_sums(lists, strip_ref, mixed_ref.at[col], odd_x, col)
        for part in range(2):
            base_ref[part] = early_ref[0, col, part] + dot(lean_ref[part], stacked)
        cols = slice(col * length, (col + 1) * length)
        terms = [
            (lists.weight_of(odd_x, col, places[at]), swept_ref.at[at])
            for at in range(col, col + 3)
        ]

        def store(rows, real, imag):
            sum_ref[0, rows, cols] = real.astype(BF16)
            sum_ref[1, rows, cols] = imag.astype(BF16)

        mix(base_ref, terms, store)
    groups = [lists.group_at(lists.window(odd_x, col)) for col in range(2)]
    turn(halves(sum_ref, slice(None)), right_ref, groups, out_ref)
    source = start_of(odd_x, HALF, 0)
    target = start_of(odd_x, 0, tile - span)
    border = start_of(odd_x, 0, span)
    for part in range(2):
        mid_ref[part, pl.ds(target, span)] = out_ref[part, pl.ds(source, span)]
        send_o_ref[part] = out_ref[part, pl.ds(border, HALF)].astype(BF16)
    row = 1 - odd_x
    for col in range(2):
        stacked = strip_sums(lists, strip_ref, mixed_ref.at[2 + col], row, col)
        for part in range(2):
            rest_ref[part, :, col * length : (col + 1) * length] = early_ref[1, col, part] + dot(
                lean_ref[part], stacked
            )
    groups = [lists.group_at(lists.window(row, col)) for col in range(2)]
    rows = pl.ds(start_of(odd_x, span, 0), HALF)
    turn(halves(rest_ref, rows), right_ref, groups, border_ref)
    for part in range(2):
        send_e_ref[part] = border_ref[part, :, : send_e_ref.shape[2]].astype(BF16)


def halves(ref, rows):
    length = ref.shape[2] // 2
    return [
        [ref[part, rows, col * length : (col + 1) * length].astype(BF16) for part in range(2)]
        for col in range(2)
    ]


def turn(blocks, right_ref, groups, out_ref):
    real, imag = 0.0, 0.0
    for col in range(2):
        m_real, m_imag = blocks[col]
        r_real, r_imag = right_ref[groups[col], col, 0], right_ref[groups[col], col, 1]
        real += dot(m_real, r_real) - dot(m_imag, r_imag)
        imag += dot(m_real, r_imag) + dot(m_imag, r_real)
    out_ref[0] = real
    out_ref[1] = imag


def join_kernel(lists, mid_ref, rest_ref, got_ref, right_ref, full_ref, sum_ref, out_ref):
    span = got_ref.shape[1]
    tile = full_ref.shape[1]
    odd_x = lists.odd_x
    rows = pl.ds(start_of(odd_x, 0, HALF), span)
    for part in range(2):
        sum_ref[part] = (rest_ref[part, rows] + got_ref[part].astype(F32)).astype(BF16)
    lists.wait()
    groups = [lists.group_at(lists.window(1 - odd_x, col)) for col in range(2)]
    turn(halves(sum_ref, slice(None)), right_ref, groups, out_ref)
    alone = tile - span
    both = slice(alone, span)
    source, target = start_of(odd_x, span - alone, 0), start_of(odd_x, span, 0)
    shared = start_of(odd_x, 0, alone)
    for part in range(2):
        full_ref[part, pl.ds(target, alone)] = out_ref[part, pl.ds(source, alone)]
        full_ref[part, both] = (
            mid_ref[part, both] + out_ref[part, pl.ds(shared, span - alone)]
        )


def border_kernel(full_ref, echo_ref, rows_e_ref, rows_o_ref, done_ref, send_e_ref, send_o_ref):
    tile = done_ref.shape[1]
    lanes = tile // 128 * 128
    odd_x = parity("gx")
    row_e = pl.ds(start_of(odd_x, tile - HALF, 0), HALF)
    row_o = pl.ds(start_of(odd_x, 0, tile - HALF), HALF)
    width = rows_e_ref.shape[2]
    for part in range(2):
        done_ref[part, row_o] = full_ref[part, row_o] + rows_o_ref[part].astype(F32)
        done_ref[part, row_e, :width] = (
            full_ref[part, row_e, :width]
            + echo_ref[part, :, :width]
            + rows_e_ref[part].astype(F32)
        )
        turned = done_ref[part, :, lanes:].T
        west = turned[tile - lanes : tile - lanes + HALF].astype(BF16)
        east = turned[tile - lanes + HALF : tile - lanes + OVER].astype(BF16)

        def store(near, away):
            send_e_ref[part] = near
            send_o_ref[part] = away

        each_way(parity("gy"), lambda: store(east, west), lambda: store(west, east))


def rotate(real, imag, cos, sin, result_ref):
    result_ref[0, 0] = (real * cos - imag * sin).astype(BF16)
    result_ref[1, 0] = (real * sin + imag * cos).astype(BF16)


def inner_kernel(full_ref, cos_ref, sin_ref, result_ref):
    rotate(full_ref[0], full_ref[1], cos_ref[...], sin_ref[...], result_ref)


def outer_kernel(
    _, full_ref, cols_e_ref, cols_o_ref, cos_ref, sin_ref, result_hbm, west_ref, east_ref, sems
):
    tile = full_ref.shape[1]
    lanes = tile // 128 * 128

    def side(cols_ref, cols, shift, out_ref):
        size = cols.stop - cols.start
        lane = lax.broadcasted_iota(jnp.int32, (HALF, size), 1)
        line = lax.broadcasted_iota(jnp.int32, (HALF, size), 0)
        pick = (lane == line + shift).astype(F32).astype(BF16)
        real, imag = (
            full_ref[part, :, cols]
            + lax.dot_general(
                cols_ref[part], pick, (((0,), (0,)), ((), ())), preferred_element_type=F32
            )
            for part in range(2)
        )
        rotate(real, imag, cos_ref[:, cols], sin_ref[:, cols], out_ref)

    west, east = slice(0, 128), slice(lanes, tile)
    copies = [
        pltpu.make_async_copy(ref, result_hbm.at[:, :, :, cols], sems.at[i])
        for i, (ref, cols) in enumerate(((west_ref, west), (east_ref, east)))
    ]

    def sides(to_west_ref, to_east_ref):
        side(to_west_ref, west, 0, west_ref)
        copies[0].start()
        side(to_east_ref, east, tile - HALF - lanes, east_ref)
        copies[1].start()

    each_way(
        parity("gy"), lambda: sides(cols_o_ref, cols_e_ref), lambda: sides(cols_e_ref, cols_o_ref)
    )
    for copy in copies:
        copy.wait()


def phase_kernel(freq_ref, slow_ref, _, cos_ref, sin_ref):
    angle = freq_ref[0] * slow_ref[...]
    turns = jnp.round(angle * (2.0 / math.pi))
    rest = angle - turns * 1.57080078125
    rest = rest + turns * 4.45445510338e-6
    square = rest * rest
    sine = rest + rest * square * (
        -1.6666654611e-1 + square * (8.3321608736e-3 - square * 1.9515295891e-4)
    )
    cosine = 1.0 - 0.5 * square + square * square * (
        4.166664568298827e-2 + square * (-1.388731625493765e-3 + square * 2.443315711809948e-5)
    )
    quarter = turns.astype(jnp.int32) & 3
    crossed = (quarter & 1) == 1
    sin_value = jnp.where(crossed, cosine, sine)
    cos_value = jnp.where(crossed, sine, cosine)
    sin_ref[...] = jnp.where(quarter >= 2, -sin_value, sin_value)
    cos_ref[...] = jnp.where((quarter == 1) | (quarter == 2), -cos_value, cos_value)


def per_device(
    wavefield, slowness, frequencies, propagator, window_velocity_group, reach_list, coupling
):
    length = propagator.shape[-1]
    span = length - HALF
    wide = 2 * length
    tile_rows, tile_cols = wavefield.shape[2:]
    slots = reach_list.shape[2]

    def shape(*dims, kind=BF16):
        return pltpu.VMEM(dims, kind)

    x_send = pl.pallas_call(
        rows_kernel,
        out_shape=shape(2, span, tile_cols + 8),
        in_specs=[VMEM],
        out_specs=VMEM,
        compiler_params=PARAMS,
        cost_estimate=cost(0.5),
        name="rows",
    )(wavefield)
    x_odd = swap(x_send, "gx", True)
    near, far, corner = pl.pallas_call(
        cols_kernel,
        out_shape=(shape(2, tile_rows, span),) * 2 + (shape(2, span, span),),
        in_specs=[VMEM] * 2,
        out_specs=(VMEM,) * 3,
        compiler_params=PARAMS,
        cost_estimate=cost(0.5),
        name="cols",
    )(wavefield, x_send)
    y_near = swap(near, "gy", False)
    y_far = swap(far, "gy", True)
    z_far = far_corner(corner)
    y_near = swap(near, "gy", False)

    left, strip, *tables = fold(
        propagator,
        cosine_table(length),
        bell_curve(length, OVER),
        reach_list,
        coupling,
        window_velocity_group,
    )
    def call(kernel, name, micros, out_shape, inputs, scratch=(), **options):
        def body(*refs):
            *refs, place_ref, weight_ref, sems = refs
            copies = fetch(((refs[0], place_ref), (refs[1], weight_ref)), sems)
            kernel(Lists(place_ref, weight_ref, copies, slots), *refs[2:])

        specs = options.pop("in_specs", [VMEM] * len(inputs))
        outs = options.pop("out_specs", jax.tree.map(lambda _: VMEM, out_shape))
        return pl.pallas_call(
            body,
            out_shape=out_shape,
            in_specs=[ANY] * 2 + specs,
            out_specs=outs,
            scratch_shapes=list(scratch)
            + [pltpu.SMEM(table.shape, table.dtype) for table in tables]
            + [pltpu.SemaphoreType.DMA((2,))],
            compiler_params=PARAMS,
            name=name,
            cost_estimate=cost(micros),
            **options,
        )(*tables, *inputs)

    right = pl.pallas_call(
        right_kernel,
        out_shape=shape(left.shape[0], 2, 2, length, wide),
        in_specs=[VMEM],
        out_specs=VMEM,
        compiler_params=PARAMS,
        cost_estimate=cost(0.01),
        name="right",
    )(left)
    frame, given, gave, swept, rim_send = call(
        edge_kernel,
        "edge",
        0.001,
        (
            shape(4, 2, tile_rows + OVER, length),
            shape(2, span, wide),
            shape(2, HALF, wide),
            shape(2, 4, 2, length, length, kind=F32),
            shape(4, 2, HALF, length),
        ),
        (wavefield, y_near, y_far, left, right),
        (pltpu.VMEM((2, length, wide), BF16),),
        in_specs=[VMEM] * 4 + [ANY],
    )
    rim = swap(rim_send, "gx", False)
    got = swap(given, "gx", False)

    cos_phase, sin_phase = pl.pallas_call(
        phase_kernel,
        out_shape=(shape(tile_rows, tile_cols, kind=F32),) * 2,
        in_specs=[SMEM, VMEM, ANY],
        out_specs=(VMEM,) * 2,
        compiler_params=PARAMS,
        cost_estimate=cost(0.01),
        name="phase",
    )(frequencies, slowness, rim_send)

    corner_near = pl.pallas_call(
        corner_kernel,
        out_shape=shape(2, span, span),
        in_specs=[VMEM, ANY],
        out_specs=VMEM,
        compiler_params=PARAMS,
        cost_estimate=cost(0.2),
        name="corner",
    )(x_odd, rim_send)
    z_near = swap(corner_near, "gy", False)
    early, echo, _ = call(
        early_kernel,
        "early",
        3,
        (
            shape(2, 2, 2, length, length, kind=F32),
            shape(2, HALF, wide, kind=F32),
            shape(2, 4, 2, length, length, kind=F32),
        ),
        (frame, left, gave, right, swept),
        input_output_aliases={6: 2},
    )
    mid, rest, send_o, send_e = call(
        late_kernel,
        "late",
        4,
        (
            shape(2, tile_rows, wide, kind=F32),
            shape(2, length, wide, kind=F32),
            shape(2, HALF, wide),
            shape(2, HALF, tile_cols + OVER),
        ),
        (x_odd, rim, z_near, z_far, left, strip, frame, early, right),
        (
            pltpu.VMEM((4, 4, 2, OVER, length), BF16),
            pltpu.VMEM((4, 2, length, length), BF16),
            pltpu.VMEM((4, 2, length, length), F32),
            pltpu.VMEM((2, length, length), F32),
            pltpu.VMEM((4, length, length), F32),
            pltpu.VMEM((2, length, wide), BF16),
            pltpu.VMEM((2, length, wide), F32),
            pltpu.VMEM((2, HALF, wide), F32),
        ),
    )
    rows_o = swap(send_o, "gx", True)
    rows_e = swap(send_e, "gx", False)
    full = call(
        join_kernel,
        "join",
        0.001,
        shape(2, tile_rows, wide, kind=F32),
        (mid, rest, got, right),
        (
            pltpu.VMEM((2, span, wide), BF16),
            pltpu.VMEM((2, span, wide), F32),
        ),
        input_output_aliases={2: 0},
    )
    full, send_e, send_o = pl.pallas_call(
        border_kernel,
        out_shape=(shape(2, tile_rows, wide, kind=F32),) + (shape(2, HALF, tile_rows),) * 2,
        in_specs=[VMEM] * 4,
        out_specs=(VMEM,) * 3,
        input_output_aliases={0: 0},
        compiler_params=PARAMS,
        cost_estimate=cost(0.5),
        name="border",
    )(full, echo, rows_e, rows_o)
    cols_o = swap(send_o, "gy", True)
    cols_e = swap(send_e, "gy", False)
    result = jax.ShapeDtypeStruct(wavefield.shape, BF16)
    count = -(-tile_cols // 128)

    def blocks(place):
        return (
            pl.BlockSpec((2, tile_rows, 128), lambda i: (0, 0, place(i))),
            pl.BlockSpec((tile_rows, 128), lambda i: (0, place(i))),
            pl.BlockSpec((2, 1, tile_rows, 128), lambda i: (0, 0, 0, place(i))),
        )

    full_spec, phase_spec, out_spec = blocks(lambda i: i + 1)
    partly = pl.pallas_call(
        inner_kernel,
        grid=(count - 2,),
        out_shape=result,
        in_specs=[full_spec, phase_spec, phase_spec],
        out_specs=out_spec,
        compiler_params=PARAMS,
        cost_estimate=cost(1),
        name="inner",
    )(full, cos_phase, sin_phase)
    return pl.pallas_call(
        outer_kernel,
        out_shape=result,
        in_specs=[ANY] + [VMEM] * 5,
        out_specs=ANY,
        scratch_shapes=[
            pltpu.VMEM((2, 1, tile_rows, 128), BF16),
            pltpu.VMEM((2, 1, tile_rows, tile_cols % 128), BF16),
            pltpu.SemaphoreType.DMA((2,)),
        ],
        input_output_aliases={0: 0},
        compiler_params=PARAMS,
        cost_estimate=cost(1),
        name="outer",
    )(partly, full, cols_e, cols_o, cos_phase, sin_phase)


def solution(mesh):
    return jax.shard_map(
        per_device,
        mesh=mesh,
        in_specs=(P(None, None, "gx", "gy"), P("gx", "gy"), P(), P(), P(), P(), P()),
        out_specs=P(None, None, "gx", "gy"),
        check_vma=False,
    )
```

```python
import functools
import math

import jax
import jax.numpy as jnp
import ml_dtypes
import numpy as np
from jax import lax
from jax.experimental import pallas as pl
from jax.experimental.pallas import tpu as pltpu
from jax.sharding import PartitionSpec as P

OVER = 32
HALF = OVER // 2
F32 = jnp.float32
BF16 = jnp.bfloat16
VMEM = pl.BlockSpec(memory_space=pltpu.VMEM)
SMEM = pl.BlockSpec(memory_space=pltpu.SMEM)
ANY = pl.BlockSpec(memory_space=pl.ANY)
PARAMS = pltpu.CompilerParams(vmem_limit_bytes=20 * 2**20)


def cosine_table(length):
    points = np.arange(length, dtype=np.float32) + np.float32(0.5)
    angles = (np.float32(math.pi / length) * points[:, None]) * points[None, :]
    waves = np.cos(angles.astype(np.float64)).astype(np.float32)
    return (np.sqrt(np.float32(2.0 / length)) * waves).astype(ml_dtypes.bfloat16)


def bell_curve(length, margin):
    points = np.arange(length, dtype=np.float64)
    rising = np.sin(0.5 * math.pi * (points + 0.5) / margin)
    falling = np.cos(0.5 * math.pi * (points - (length - margin) + 0.5) / margin)
    bell = np.where(points < margin, rising, np.where(points >= length - margin, falling, 1.0))
    return bell.astype(np.float32)


def dot(left, right):
    return jnp.dot(left, right, preferred_element_type=F32)


def swap(block, axis, odd):
    size = lax.axis_size(axis)
    pairs = []
    for i in range(1 if odd else 0, size - 1, 2):
        pairs += [(i, i + 1), (i + 1, i)]
    return lax.ppermute(block, axis, pairs)


def far_corner(block):
    across, along = (lax.axis_size(axis) for axis in ("gx", "gy"))
    pairs = []
    for x in range(1, across - 1, 2):
        for y in range(1, along - 1, 2):
            first, second = x * along + y, (x + 1) * along + y + 1
            third, fourth = x * along + y + 1, (x + 1) * along + y
            pairs += [(first, second), (second, first), (third, fourth), (fourth, third)]
    return lax.ppermute(block, ("gx", "gy"), pairs)


def parity(axis):
    return lax.rem(lax.axis_index(axis), 2)


def cost(micros):
    return pl.CostEstimate(
        flops=int(micros * 1.1e9), bytes_accessed=int(micros * 3.6e6), transcendentals=0
    )


def fetch(pairs, sems):
    copies = [pltpu.make_async_copy(a, b, sems.at[i]) for i, (a, b) in enumerate(pairs)]
    for copy in copies:
        copy.start()
    return copies


def list_tables(all_reach_ref, all_coup_ref, all_group_ref, place_ref, weight_ref):
    slots, total_y, total_x = all_reach_ref.shape
    odd_x = parity("gx")
    base_x = lax.axis_index("gx") * 2
    base_y = lax.axis_index("gy") * 2
    for row in range(4):
        for col in range(4):
            x = jnp.clip(base_x - 1 + row, 0, total_x - 1)
            y = jnp.clip(base_y - 1 + col, 0, total_y - 1)
            place_ref[row * 4 + col] = all_group_ref[y, x]
    for row in range(3):
        for col in range(2):
            x, y = base_x - odd_x + row, base_y + col
            here = (row - odd_x + 1) * 4 + col + 1
            for slot in range(slots):
                reach = all_reach_ref[slot, y, x]
                step = reach - (x * total_y + y)
                down = jnp.where(step > 1, 1, jnp.where(step < -1, -1, 0))
                place = here + step + down * (4 - total_y)
                at = (row * 2 + col) * slots + slot
                place_ref[16 + at] = jnp.where(reach >= 0, place, -1)
                weight_ref[at * 2] = all_coup_ref[col, slot, 0, x]
                weight_ref[at * 2 + 1] = all_coup_ref[col, slot, 1, x]


def folded_kernel(
    reach_any,
    coup_any,
    group_any,
    prop_ref,
    cos_ref,
    cos_t_ref,
    row_ref,
    left_ref,
    strip_ref,
    place_any,
    weight_any,
    reach_ref,
    coup_ref,
    group_ref,
    place_ref,
    weight_ref,
    sems,
):
    columns = pl.ds(lax.axis_index("gy") * 2, 2)
    pairs = ((reach_any, reach_ref), (coup_any.at[columns], coup_ref), (group_any, group_ref))
    copies = fetch(pairs, sems)
    groups, _, _, length, _ = prop_ref.shape
    strip_ref[...] = jnp.zeros_like(strip_ref)
    curve = jnp.broadcast_to(row_ref[...], (length, length))
    bell = curve * curve.T
    edge = length - HALF
    for g in range(groups):
        if g == groups - 1:
            for copy in copies:
                copy.wait()
            list_tables(reach_ref, coup_ref, group_ref, place_ref, weight_ref)
            outward = fetch(((place_ref, place_any), (weight_ref, weight_any)), sems.at[3:])
        for part in range(2):
            half = dot(prop_ref[g, 0, part], cos_ref[...])
            high = half.astype(BF16)
            low = (half - high.astype(F32)).astype(BF16)
            full = (dot(cos_t_ref[...], high) + dot(cos_t_ref[...], low)) * bell
            left_ref[g, part] = full.astype(BF16)
            strip = jnp.concatenate([full[:, :HALF], full[:, edge:]], axis=1).astype(BF16)
            low = slice(g * OVER, (g + 1) * OVER)
            high = slice(length // 2 + g * OVER, length // 2 + (g + 1) * OVER)
            strip_ref[part, :, low] = strip
            strip_ref[1 - part, :, high] = strip if part == 0 else -strip
    for copy in outward:
        copy.wait()

def right_kernel(left_ref, right_ref):
    groups, _, length, _ = left_ref.shape
    wide = right_ref.shape[-1]
    inner = wide - 2 * OVER
    edge = length - HALF
    zeros = jnp.zeros((length, wide), BF16)
    for g in range(groups):
        for part in range(2):
            flipped = left_ref[g, part].astype(F32).T.astype(BF16)
            right_ref[g, 0, part] = jnp.concatenate(
                [
                    flipped[:, HALF:],
                    zeros[:, : inner - edge],
                    flipped[:, :HALF],
                    zeros[:, : wide - inner - HALF],
                ],
                axis=1,
            )
            right_ref[g, 1, part] = jnp.concatenate(
                [
                    zeros[:, : inner - edge],
                    flipped[:, :edge],
                    zeros[:, :HALF],
                    flipped[:, edge:],
                    zeros[:, : wide - inner - OVER],
                ],
                axis=1,
            )


def fold(propagator, cosines, bell, reach_list, coupling, window_velocity_group):
    groups, _, _, length, _ = propagator.shape
    slots = reach_list.shape[2]
    entries = 6 * slots
    return pl.pallas_call(
        folded_kernel,
        out_shape=(
            pltpu.VMEM((groups, 2, length, length), BF16),
            pltpu.VMEM((2, length, length), BF16),
            jax.ShapeDtypeStruct((16 + entries,), jnp.int32),
            jax.ShapeDtypeStruct((2 * entries,), F32),
        ),
        in_specs=[ANY] * 3 + [VMEM] * 4,
        out_specs=(VMEM,) * 2 + (ANY,) * 2,
        scratch_shapes=[
            pltpu.SMEM(reach_list.shape[::-1], jnp.int32),
            pltpu.SMEM((2, slots, 2, coupling.shape[0]), F32),
            pltpu.SMEM(window_velocity_group.shape[::-1], jnp.int32),
            pltpu.SMEM((16 + entries,), jnp.int32),
            pltpu.SMEM((2 * entries,), F32),
            pltpu.SemaphoreType.DMA((5,)),
        ],
        compiler_params=PARAMS,
        cost_estimate=cost(0.1),
        name="fold",
    )(
        jnp.transpose(reach_list, (2, 1, 0)),
        jnp.transpose(coupling, (1, 2, 3, 0)),
        window_velocity_group.T,
        propagator,
        cosines,
        cosines.T,
        bell[None, :],
    )


def spread(west, middle, east, part):
    span = west.shape[2]
    wide = 2 * (span - HALF)
    left, centre, right = west[part], middle[part], east[part]
    return (
        jnp.concatenate([left, centre[:, :HALF]], axis=1),
        jnp.concatenate([left[:, span - HALF :], centre[:, :span]], axis=1),
        jnp.concatenate([centre[:, wide - span : wide], right[:, :HALF]], axis=1),
        jnp.concatenate([centre[:, wide - HALF : wide], right], axis=1),
    )


def each_way(odd, even_call, odd_call):
    pl.when(odd == 0)(even_call)
    pl.when(odd == 1)(odd_call)


def start_of(odd, if_even, if_odd):
    return pl.multiple_of(jnp.where(odd == 0, if_even, if_odd), HALF)


def sweep(matrix_ref, x_real, x_imag, out_ref):
    t_real, t_imag = matrix_ref[0], matrix_ref[1]
    out_ref[0] = dot(t_real, x_real) - dot(t_imag, x_imag)
    out_ref[1] = dot(t_real, x_imag) + dot(t_imag, x_real)


def mix(base_ref, terms, store):
    length = terms[0][1].shape[1]
    for start in range(0, length, OVER):
        rows = slice(start, start + OVER)
        real, imag = (0.0, 0.0) if base_ref is None else (base_ref[0, rows], base_ref[1, rows])
        for (w_real, w_imag), ref in terms:
            u_real, u_imag = ref[0, rows], ref[1, rows]
            real += w_real * u_real - w_imag * u_imag
            imag += w_real * u_imag + w_imag * u_real
        store(rows, real, imag)


class Lists:
    def __init__(self, place_ref, weight_ref, copies, slots):
        self.place_ref, self.weight_ref = place_ref, weight_ref
        self.copies, self.slots = copies, slots
        self.odd_x = parity("gx")

    def wait(self):
        for copy in self.copies:
            copy.wait()

    def group_at(self, place):
        return self.place_ref[place]

    def window(self, row, col):
        return (row + 1) * 4 + col + 1

    def entry(self, row, col, slot):
        at = ((row + self.odd_x) * 2 + col) * self.slots + slot
        return self.place_ref[16 + at], self.weight_ref[at * 2], self.weight_ref[at * 2 + 1]

    def weight_of(self, row, col, source):
        real, imag = jnp.float32(0), jnp.float32(0)
        for slot in range(self.slots):
            reach, c_real, c_imag = self.entry(row, col, slot)
            real += jnp.where(reach == source, c_real, 0.0)
            imag += jnp.where(reach == source, c_imag, 0.0)
        return real, imag

    def slot_of(self, row, col, slot):
        reach, c_real, c_imag = self.entry(row, col, slot)
        live = reach >= 0
        source = jnp.where(live, reach, self.window(row, col))
        at_row = source >> 2
        at_x = jnp.where(self.odd_x == 0, at_row, 3 - at_row)
        real = jnp.where(live, c_real, 0.0)
        imag = jnp.where(live, c_imag, 0.0)
        return self.group_at(source), at_x, source & 3, real, imag


def pack_sides(block, near_ref, far_ref):
    width = near_ref.shape[2]
    start = block.shape[2] - width

    def store(high_ref, low_ref):
        high_ref[...] = block[:, :, start:]
        low_ref[...] = block[:, :, :width]

    each_way(parity("gy"), lambda: store(near_ref, far_ref), lambda: store(far_ref, near_ref))


def rows_kernel(wave_ref, x_ref):
    tile, span = wave_ref.shape[2], x_ref.shape[1]
    for part in range(2):
        rows = pl.ds(start_of(parity("gx"), 0, tile - span), span)
        x_ref[part, :, :tile] = wave_ref[part, 0, rows]
        x_ref[part, :, tile:] = jnp.zeros((span, x_ref.shape[2] - tile), BF16)


def cols_kernel(wave_ref, _, near_ref, far_ref, corner_ref):
    pack_sides(wave_ref.at[:, 0], near_ref, far_ref)
    span = corner_ref.shape[1]
    rows = pl.ds(start_of(parity("gx"), 0, wave_ref.shape[2] - span), span)
    corner_ref[...] = far_ref[:, rows]


def corner_kernel(x_ref, _, near_ref):
    width = near_ref.shape[2]
    start = 2 * (width - HALF) - width

    def store(cols):
        near_ref[...] = x_ref[:, :, cols]

    each_way(
        parity("gy"), lambda: store(slice(start, start + width)), lambda: store(slice(0, width))
    )


def window_rows(odd_x, at_x, length):
    return pl.multiple_of(jnp.where((at_x == 1) == (odd_x == 0), 0, length - OVER), HALF)


def fill_frame(frame_ref, wave_ref, ye_ref, yo_ref):
    tile = wave_ref.shape[2]
    rim = jnp.zeros((HALF, frame_ref.shape[3]), BF16)

    def fill(west, east):
        for part in range(2):
            for at, block in enumerate(spread(west, wave_ref.at[:, 0], east, part)):
                frame_ref[at, part, HALF : HALF + tile] = block
                frame_ref[at, part, :HALF] = rim
                frame_ref[at, part, HALF + tile :] = rim

    each_way(parity("gy"), lambda: fill(yo_ref, ye_ref), lambda: fill(ye_ref, yo_ref))


def edge_kernel(
    lists,
    wave_ref,
    ye_ref,
    yo_ref,
    left_ref,
    right_ref,
    frame_ref,
    send_ref,
    echo_ref,
    swept_ref,
    rim_ref,
    part_ref,
    out_ref,
):
    length = left_ref.shape[-1]
    tile = wave_ref.shape[2]
    fill_frame(frame_ref, wave_ref, ye_ref, yo_ref)
    edge = pl.ds(start_of(lists.odd_x, tile, HALF), HALF)
    for at in range(4):
        for part in range(2):
            rim_ref[at, part] = frame_ref[at, part, edge]
    lists.wait()
    beyond = jnp.where(lists.odd_x == 0, 2, -1)
    mine = jnp.where(lists.odd_x == 0, 1, 0)
    rows = pl.ds(window_rows(lists.odd_x, 2, length), length)
    places = [lists.window(mine, at - 1) for at in range(4)]
    for at, place in enumerate(places):
        matrix_ref = left_ref.at[lists.group_at(place)]
        sweep(matrix_ref, frame_ref[at, 0, rows], frame_ref[at, 1, rows], swept_ref.at[1, at])
    for col in range(2):
        cols = slice(col * length, (col + 1) * length)
        terms = [
            (lists.weight_of(beyond, col, places[at]), swept_ref.at[1, at])
            for at in range(col, col + 3)
        ]

        def store(rows, real, imag):
            part_ref[0, rows, cols] = real.astype(BF16)
            part_ref[1, rows, cols] = imag.astype(BF16)

        mix(None, terms, store)
    groups = [lists.group_at(lists.window(beyond, col)) for col in range(2)]
    turn(halves(part_ref, slice(None)), right_ref, groups, out_ref)
    span = length - HALF
    inner, outer = start_of(lists.odd_x, HALF, 0), start_of(lists.odd_x, 0, span)
    for part in range(2):
        send_ref[part] = out_ref[part, pl.ds(inner, span), : send_ref.shape[2]].astype(BF16)
        echo_ref[part] = out_ref[part, pl.ds(outer, HALF)]


def early_kernel(lists, frame_ref, left_ref, _, sum_ref, swept_ref):
    length = left_ref.shape[-1]
    lists.wait()
    rows = pl.ds(window_rows(lists.odd_x, 1, length), length)
    for at in range(4):
        matrix_ref = left_ref.at[lists.group_at(lists.window(lists.odd_x, at - 1))]
        sweep(matrix_ref, frame_ref[at, 0, rows], frame_ref[at, 1, rows], swept_ref.at[0, at])
    for c in range(2):
        for col in range(2):
            terms = []
            for slot in range(lists.slots):
                _, at_x, at_y, w_real, w_imag = lists.slot_of(lists.odd_x ^ c, col, slot)
                inside = (at_x == 1) | (at_x == 2)
                weight = jnp.where(inside, w_real, 0.0), jnp.where(inside, w_imag, 0.0)
                terms.append((weight, swept_ref.at[jnp.clip(at_x - 1, 0, 1), at_y]))

            def store(rows, real, imag):
                sum_ref[c, col, 0, rows] = real
                sum_ref[c, col, 1, rows] = imag

            mix(None, terms, store)


def mix_slots(mixed_ref, groups, weights, pieces):
    half = mixed_ref.shape[0] // 2
    for group, (w_real, w_imag), (real, imag) in zip(groups, weights, pieces):
        real, imag = real.astype(F32), imag.astype(F32)
        at = pl.multiple_of(group * OVER, OVER)
        mixed_ref[pl.ds(at, OVER)] += w_real * real - w_imag * imag
        mixed_ref[pl.ds(half + at, OVER)] += w_real * imag + w_imag * real


def strip_sums(lists, strip_ref, mixed_ref, row, col):
    mixed_ref[...] = jnp.zeros_like(mixed_ref)
    groups, weights, pieces = [], [], []
    for slot in range(lists.slots):
        group, at_x, at_y, w_real, w_imag = lists.slot_of(row, col, slot)
        groups.append(group)
        weights.append((w_real, w_imag))
        pieces.append((strip_ref[at_x, at_y, 0], strip_ref[at_x, at_y, 1]))
    mix_slots(mixed_ref, groups, weights, pieces)
    return mixed_ref[...].astype(BF16)


def late_kernel(
    lists,
    xo_ref,
    rim_ref,
    ze_ref,
    zo_ref,
    left_ref,
    lean_ref,
    frame_ref,
    early_ref,
    right_ref,
    mid_ref,
    send_o_ref,
    send_e_ref,
    strip_ref,
    outer_ref,
    swept_ref,
    base_ref,
    mixed_ref,
    sum_ref,
    out_ref,
    rest_ref,
    even_ref,
):
    length = left_ref.shape[-1]
    span = length - HALF
    tile = mid_ref.shape[1]
    odd_x, odd_y = lists.odd_x, parity("gy")
    at_o, hole_o = start_of(odd_x, 0, HALF), start_of(odd_x, span, 0)
    lean_o, lean_e = start_of(odd_x, 0, HALF), start_of(odd_x, HALF, 0)
    strip_ref[...] = jnp.zeros_like(strip_ref)

    def fill(west, east):
        for part in range(2):
            for at, block in enumerate(spread(west, xo_ref, east, part)):
                outer_ref[at, part, pl.ds(at_o, span)] = block
                outer_ref[at, part, pl.ds(hole_o, HALF)] = jnp.zeros((HALF, length), BF16)
                strip_ref[2, at, part, pl.ds(lean_e, HALF)] = rim_ref[at, part]

    each_way(odd_y, lambda: fill(zo_ref, ze_ref), lambda: fill(ze_ref, zo_ref))
    shift = start_of(odd_x, span - HALF, HALF)
    near_o, near_e = start_of(odd_x, HALF, tile), start_of(odd_x, tile, HALF)
    for at in range(4):
        for part in range(2):
            strip_ref[1, at, part, pl.ds(lean_o, HALF)] = outer_ref[at, part, pl.ds(shift, HALF)]
            strip_ref[0, at, part, pl.ds(lean_e, HALF)] = frame_ref[at, part, pl.ds(near_o, HALF)]
            strip_ref[3, at, part, pl.ds(lean_o, HALF)] = frame_ref[at, part, pl.ds(near_e, HALF)]

    lists.wait()
    beyond = jnp.where(odd_x == 0, -1, 2)
    places = [lists.window(beyond, at - 1) for at in range(4)]
    for at, place in enumerate(places):
        matrix_ref = left_ref.at[lists.group_at(place)]
        sweep(matrix_ref, outer_ref[at, 0], outer_ref[at, 1], swept_ref.at[at])
    for col in range(2):
        stacked = strip_sums(lists, strip_ref, mixed_ref.at[col], odd_x, col)
        for part in range(2):
            base_ref[part] = early_ref[0, col, part] + dot(lean_ref[part], stacked)
        cols = slice(col * length, (col + 1) * length)
        terms = [
            (lists.weight_of(odd_x, col, places[at]), swept_ref.at[at])
            for at in range(col, col + 3)
        ]

        def store(rows, real, imag):
            sum_ref[0, rows, cols] = real.astype(BF16)
            sum_ref[1, rows, cols] = imag.astype(BF16)

        mix(base_ref, terms, store)
    groups = [lists.group_at(lists.window(odd_x, col)) for col in range(2)]
    turn(halves(sum_ref, slice(None)), right_ref, groups, out_ref)
    source = start_of(odd_x, HALF, 0)
    target = start_of(odd_x, 0, tile - span)
    border = start_of(odd_x, 0, span)
    for part in range(2):
        mid_ref[part, pl.ds(target, span)] = out_ref[part, pl.ds(source, span)]
        send_o_ref[part] = out_ref[part, pl.ds(border, HALF)].astype(BF16)
    row = 1 - odd_x
    for col in range(2):
        stacked = strip_sums(lists, strip_ref, mixed_ref.at[2 + col], row, col)
        for part in range(2):
            rest_ref[part, :, col * length : (col + 1) * length] = (
                early_ref[1, col, part] + dot(lean_ref[part], stacked)
            ).astype(BF16)
    groups = [lists.group_at(lists.window(row, col)) for col in range(2)]
    turn(halves(rest_ref, slice(None)), right_ref, groups, even_ref)
    border = start_of(odd_x, span, 0)
    alone = tile - span
    both = slice(alone, span)
    source, target = start_of(odd_x, span - alone, HALF), start_of(odd_x, span, 0)
    shared = start_of(odd_x, 0, HALF + alone)
    for part in range(2):
        mid_ref[part, pl.ds(target, alone)] = even_ref[part, pl.ds(source, alone)]
        mid_ref[part, both] += even_ref[part, pl.ds(shared, span - alone)]
        send_e_ref[part] = even_ref[part, pl.ds(border, HALF), : send_e_ref.shape[2]].astype(BF16)


def halves(ref, rows):
    length = ref.shape[2] // 2
    return [
        [ref[part, rows, col * length : (col + 1) * length].astype(BF16) for part in range(2)]
        for col in range(2)
    ]


def turn(blocks, right_ref, groups, out_ref):
    real, imag = 0.0, 0.0
    for col in range(2):
        m_real, m_imag = blocks[col]
        r_real, r_imag = right_ref[groups[col], col, 0], right_ref[groups[col], col, 1]
        real += dot(m_real, r_real) - dot(m_imag, r_imag)
        imag += dot(m_real, r_imag) + dot(m_imag, r_real)
    out_ref[0] = real
    out_ref[1] = imag


def join_kernel(
    mid_ref, got_ref, echo_ref, rows_e_ref, rows_o_ref, full_ref, send_e_ref, send_o_ref
):
    span, width = got_ref.shape[1:]
    tile = full_ref.shape[1]
    odd_x = parity("gx")
    rows = pl.ds(start_of(odd_x, tile - span, 0), span)
    row_e = pl.ds(start_of(odd_x, tile - HALF, 0), HALF)
    row_o = pl.ds(start_of(odd_x, 0, tile - HALF), HALF)
    lanes = tile // 128 * 128
    for part in range(2):
        full_ref[part, rows, :width] = mid_ref[part, rows, :width] + got_ref[part].astype(F32)
        full_ref[part, row_o] = mid_ref[part, row_o] + rows_o_ref[part].astype(F32)
        full_ref[part, row_e, :width] += echo_ref[part, :, :width] + rows_e_ref[part].astype(F32)
        turned = full_ref[part, :, lanes:].T
        west = turned[tile - lanes : tile - lanes + HALF].astype(BF16)
        east = turned[tile - lanes + HALF : tile - lanes + OVER].astype(BF16)

        def store(near, away):
            send_e_ref[part] = near
            send_o_ref[part] = away

        each_way(parity("gy"), lambda: store(east, west), lambda: store(west, east))


def rotate(real, imag, cos, sin, result_ref):
    result_ref[0, 0] = (real * cos - imag * sin).astype(BF16)
    result_ref[1, 0] = (real * sin + imag * cos).astype(BF16)


def inner_kernel(full_ref, cos_ref, sin_ref, result_ref):
    rotate(full_ref[0], full_ref[1], cos_ref[...], sin_ref[...], result_ref)


def outer_kernel(
    _, full_ref, cols_e_ref, cols_o_ref, cos_ref, sin_ref, result_hbm, west_ref, east_ref, sems
):
    tile = full_ref.shape[1]
    lanes = tile // 128 * 128

    def side(cols_ref, cols, shift, out_ref):
        size = cols.stop - cols.start
        lane = lax.broadcasted_iota(jnp.int32, (HALF, size), 1)
        line = lax.broadcasted_iota(jnp.int32, (HALF, size), 0)
        pick = (lane == line + shift).astype(F32).astype(BF16)
        real, imag = (
            full_ref[part, :, cols]
            + lax.dot_general(
                cols_ref[part], pick, (((0,), (0,)), ((), ())), preferred_element_type=F32
            )
            for part in range(2)
        )
        rotate(real, imag, cos_ref[:, cols], sin_ref[:, cols], out_ref)

    west, east = slice(0, 128), slice(lanes, tile)
    copies = [
        pltpu.make_async_copy(ref, result_hbm.at[:, :, :, cols], sems.at[i])
        for i, (ref, cols) in enumerate(((west_ref, west), (east_ref, east)))
    ]

    def sides(to_west_ref, to_east_ref):
        side(to_west_ref, west, 0, west_ref)
        copies[0].start()
        side(to_east_ref, east, tile - HALF - lanes, east_ref)
        copies[1].start()

    each_way(
        parity("gy"), lambda: sides(cols_o_ref, cols_e_ref), lambda: sides(cols_e_ref, cols_o_ref)
    )
    for copy in copies:
        copy.wait()


def phase_kernel(freq_ref, slow_ref, _, cos_ref, sin_ref):
    angle = freq_ref[0] * slow_ref[...]
    turns = jnp.round(angle * (2.0 / math.pi))
    rest = angle - turns * 1.57080078125
    rest = rest + turns * 4.45445510338e-6
    square = rest * rest
    sine = rest + rest * square * (
        -1.6666654611e-1 + square * (8.3321608736e-3 - square * 1.9515295891e-4)
    )
    cosine = 1.0 - 0.5 * square + square * square * (
        4.166664568298827e-2 + square * (-1.388731625493765e-3 + square * 2.443315711809948e-5)
    )
    quarter = turns.astype(jnp.int32) & 3
    crossed = (quarter & 1) == 1
    sin_value = jnp.where(crossed, cosine, sine)
    cos_value = jnp.where(crossed, sine, cosine)
    sin_ref[...] = jnp.where(quarter >= 2, -sin_value, sin_value)
    cos_ref[...] = jnp.where((quarter == 1) | (quarter == 2), -cos_value, cos_value)


def per_device(
    wavefield, slowness, frequencies, propagator, window_velocity_group, reach_list, coupling
):
    length = propagator.shape[-1]
    span = length - HALF
    wide = 2 * length
    tile_rows, tile_cols = wavefield.shape[2:]
    slots = reach_list.shape[2]

    def shape(*dims, kind=BF16):
        return pltpu.VMEM(dims, kind)

    x_send = pl.pallas_call(
        rows_kernel,
        out_shape=shape(2, span, tile_cols + 8),
        in_specs=[VMEM],
        out_specs=VMEM,
        compiler_params=PARAMS,
        cost_estimate=cost(0.5),
        name="rows",
    )(wavefield)
    x_odd = swap(x_send, "gx", True)
    near, far, corner = pl.pallas_call(
        cols_kernel,
        out_shape=(shape(2, tile_rows, span),) * 2 + (shape(2, span, span),),
        in_specs=[VMEM] * 2,
        out_specs=(VMEM,) * 3,
        compiler_params=PARAMS,
        cost_estimate=cost(0.5),
        name="cols",
    )(wavefield, x_send)
    y_near = swap(near, "gy", False)
    y_far = swap(far, "gy", True)
    z_far = far_corner(corner)
    y_near = swap(near, "gy", False)

    left, strip, *tables = fold(
        propagator,
        cosine_table(length),
        bell_curve(length, OVER),
        reach_list,
        coupling,
        window_velocity_group,
    )
    def call(kernel, name, micros, out_shape, inputs, scratch=(), **options):
        def body(*refs):
            *refs, place_ref, weight_ref, sems = refs
            copies = fetch(((refs[0], place_ref), (refs[1], weight_ref)), sems)
            kernel(Lists(place_ref, weight_ref, copies, slots), *refs[2:])

        specs = options.pop("in_specs", [VMEM] * len(inputs))
        outs = options.pop("out_specs", jax.tree.map(lambda _: VMEM, out_shape))
        return pl.pallas_call(
            body,
            out_shape=out_shape,
            in_specs=[ANY] * 2 + specs,
            out_specs=outs,
            scratch_shapes=list(scratch)
            + [pltpu.SMEM(table.shape, table.dtype) for table in tables]
            + [pltpu.SemaphoreType.DMA((2,))],
            compiler_params=PARAMS,
            name=name,
            cost_estimate=cost(micros),
            **options,
        )(*tables, *inputs)

    right = pl.pallas_call(
        right_kernel,
        out_shape=shape(left.shape[0], 2, 2, length, wide),
        in_specs=[VMEM],
        out_specs=VMEM,
        compiler_params=PARAMS,
        cost_estimate=cost(0.01),
        name="right",
    )(left)
    frame, given, echo, swept, rim_send = call(
        edge_kernel,
        "edge",
        0.001,
        (
            shape(4, 2, tile_rows + OVER, length),
            shape(2, span, tile_cols + OVER),
            shape(2, HALF, wide, kind=F32),
            shape(2, 4, 2, length, length, kind=F32),
            shape(4, 2, HALF, length),
        ),
        (wavefield, y_near, y_far, left, right),
        (pltpu.VMEM((2, length, wide), BF16), pltpu.VMEM((2, length, wide), F32)),
    )
    rim = swap(rim_send, "gx", False)
    got = swap(given, "gx", False)

    cos_phase, sin_phase = pl.pallas_call(
        phase_kernel,
        out_shape=(shape(tile_rows, tile_cols, kind=F32),) * 2,
        in_specs=[SMEM, VMEM, ANY],
        out_specs=(VMEM,) * 2,
        compiler_params=PARAMS,
        cost_estimate=cost(0.01),
        name="phase",
    )(frequencies, slowness, rim_send)

    corner_near = pl.pallas_call(
        corner_kernel,
        out_shape=shape(2, span, span),
        in_specs=[VMEM, ANY],
        out_specs=VMEM,
        compiler_params=PARAMS,
        cost_estimate=cost(0.2),
        name="corner",
    )(x_odd, rim_send)
    z_near = swap(corner_near, "gy", False)
    early, _ = call(
        early_kernel,
        "early",
        3,
        (
            shape(2, 2, 2, length, length, kind=F32),
            shape(2, 4, 2, length, length, kind=F32),
        ),
        (frame, left, swept),
        input_output_aliases={4: 1},
    )
    mid, send_o, send_e = call(
        late_kernel,
        "late",
        4,
        (
            shape(2, tile_rows, wide, kind=F32),
            shape(2, HALF, wide),
            shape(2, HALF, tile_cols + OVER),
        ),
        (x_odd, rim, z_near, z_far, left, strip, frame, early, right),
        (
            pltpu.VMEM((4, 4, 2, OVER, length), BF16),
            pltpu.VMEM((4, 2, length, length), BF16),
            pltpu.VMEM((4, 2, length, length), F32),
            pltpu.VMEM((2, length, length), F32),
            pltpu.VMEM((4, length, length), F32),
            pltpu.VMEM((2, length, wide), BF16),
            pltpu.VMEM((2, length, wide), F32),
            pltpu.VMEM((2, length, wide), BF16),
            pltpu.VMEM((2, length, wide), F32),
        ),
    )
    rows_o = swap(send_o, "gx", True)
    rows_e = swap(send_e, "gx", False)
    full, send_e, send_o = pl.pallas_call(
        join_kernel,
        out_shape=(
            shape(2, tile_rows, wide, kind=F32),
            shape(2, HALF, tile_rows),
            shape(2, HALF, tile_rows),
        ),
        in_specs=[VMEM] * 5,
        out_specs=(VMEM,) * 3,
        input_output_aliases={0: 0},
        compiler_params=PARAMS,
        cost_estimate=cost(0.001),
        name="join",
    )(mid, got, echo, rows_e, rows_o)
    cols_o = swap(send_o, "gy", True)
    cols_e = swap(send_e, "gy", False)
    result = jax.ShapeDtypeStruct(wavefield.shape, BF16)
    count = -(-tile_cols // 128)

    def blocks(place):
        return (
            pl.BlockSpec((2, tile_rows, 128), lambda i: (0, 0, place(i))),
            pl.BlockSpec((tile_rows, 128), lambda i: (0, place(i))),
            pl.BlockSpec((2, 1, tile_rows, 128), lambda i: (0, 0, 0, place(i))),
        )

    full_spec, phase_spec, out_spec = blocks(lambda i: i + 1)
    partly = pl.pallas_call(
        inner_kernel,
        grid=(count - 2,),
        out_shape=result,
        in_specs=[full_spec, phase_spec, phase_spec],
        out_specs=out_spec,
        compiler_params=PARAMS,
        cost_estimate=cost(1),
        name="inner",
    )(full, cos_phase, sin_phase)
    return pl.pallas_call(
        outer_kernel,
        out_shape=result,
        in_specs=[ANY] + [VMEM] * 5,
        out_specs=ANY,
        scratch_shapes=[
            pltpu.VMEM((2, 1, tile_rows, 128), BF16),
            pltpu.VMEM((2, 1, tile_rows, tile_cols % 128), BF16),
            pltpu.SemaphoreType.DMA((2,)),
        ],
        input_output_aliases={0: 0},
        compiler_params=PARAMS,
        cost_estimate=cost(1),
        name="outer",
    )(partly, full, cols_e, cols_o, cos_phase, sin_phase)


def solution(mesh):
    return jax.shard_map(
        per_device,
        mesh=mesh,
        in_specs=(P(None, None, "gx", "gy"), P("gx", "gy"), P(), P(), P(), P(), P()),
        out_specs=P(None, None, "gx", "gy"),
        check_vma=False,
    )
```
